32 devices in a mesh: section: 2 (over core), dp: 4 (over z), tensor: 4 (over y, x).
Axes of the slice: x: 2, y: 2, z: 4, core: 2. Of those that a mesh axis runs over, the one named last changes fastest.
Arguments:
- tokens: bfloat16 [2, 2688, 768], P(None, ('dp', 'tensor')), may hold values from -6 to 6
- cotangent: bfloat16 [2, 2688, 768], P(None, ('dp', 'tensor')), may hold values from -6 to 6
- lengths: int32 [4, 6], P('dp'), may hold values from 0 to 325, as said below
- assignment: int32 [4, 6], P('dp'), may hold values from 0 to 1, as said below
- mix_weight: bfloat16 [2, 3, 768, 768], P('section', None, 'dp', 'tensor'), may hold values from -0.21875 to 0.21875
- head_bias: bfloat16 [2, 2, 12, 64], P('section', None, 'tensor'), may hold values from -3 to 3
- out_weight: bfloat16 [2, 768, 768], P('section', 'tensor', 'dp'), may hold values from -1.75 to 1.75
- norm_gain: bfloat16 [2, 2, 768], P('section'), may hold values from 0.25 to 1.75
- row_shift: bfloat16 [2, 4, 768], P('section'), may hold values from -2 to 2
- up_weight: bfloat16 [2, 768, 3072], P('section', 'dp', 'tensor'), may hold values from -0.21875 to 0.21875
- hidden_bias: bfloat16 [2, 24, 128], P('section', 'tensor'), may hold values from -3 to 3
- down_weight: bfloat16 [2, 3072, 768], P('section', 'tensor', 'dp'), may hold values from -0.109375 to 0.109375
Outputs:
- layer_output: bfloat16 [2, 2, 2688, 768], P('section', None, ('dp', 'tensor'))
- input_gradient: float32 [2, 2, 2688, 768], P('section', None, ('dp', 'tensor'))
- mix_gradient: float32 [2, 3, 768, 768], P('section', None, 'dp', 'tensor')
- head_gradient: float32 [2, 2, 12, 64], P('section', None, 'tensor', 'dp')
- out_gradient: float32 [2, 768, 768], P('section', 'tensor', 'dp')
- gain_gradient: float32 [2, 2, 768], P('section', None, ('dp', 'tensor'))
- shift_gradient: float32 [2, 4, 768], P('section', None, ('dp', 'tensor'))
- up_gradient: float32 [2, 768, 3072], P('section', 'dp', 'tensor')
- hidden_gradient: float32 [2, 24, 128], P('section', 'tensor', 'dp')
- down_gradient: float32 [2, 3072, 768], P('section', 'tensor', 'dp')
The draws below stay inside these ranges and needn't reach their ends.
Inputs may be any that keep to these rules, and one draw needn't show every extreme that they name: `lengths`: every slot holds an image of 197 or 325 rows, or is empty (0); the images that one group gives one micro-batch take at most 650 rows, and in every group some micro-batch takes exactly that many. `assignment`: every micro-batch has exactly three slots in each group.
All inputs are finite; a program needn't handle non-finite values.
Results may differ from the reference program's by a relative error of at most 0.018.
Values may be sent and summed in bfloat16 or wider, within the bound.
No kernel may reach another device: no remote copies, remote signals or barrier semaphores. Data moves between devices by JAX's collectives and lax.ppermute only.
A program may use at most 128 MiB of HBM per device.

```python
import jax
import jax.numpy as jnp
from jax import lax

D = 768
HEADS = 12
HEAD_DIM = 64
FF = 3072
SHORT = 197
LONG = 325
CAP = 672
MICRO = 2
SLOTS = 6
GROUPS = 4
ROWS = 2688


def layout(key):
    patterns = jnp.array([[LONG, LONG, 0], [SHORT, SHORT, SHORT], [LONG, SHORT, 0]], dtype=jnp.int32)
    kinds = jax.random.randint(jax.random.fold_in(key, 1), (GROUPS, MICRO), 0, 3)
    forced = jax.random.randint(jax.random.fold_in(key, 2), (GROUPS, 1), 0, MICRO)
    kinds = jnp.where(jnp.arange(MICRO)[None, :] == forced, 0, kinds)
    sizes = patterns[kinds].reshape(GROUPS, SLOTS)
    owners = jnp.broadcast_to(jnp.repeat(jnp.arange(MICRO, dtype=jnp.int32), 3)[None, :], (GROUPS, SLOTS))
    noise = jax.random.randint(jax.random.fold_in(key, 3), (GROUPS, SLOTS), 0, 4096)
    shuffle = jnp.argsort(noise * SLOTS + jnp.arange(SLOTS)[None, :], axis=1, stable=True)
    return (jnp.take_along_axis(sizes, shuffle, axis=1), jnp.take_along_axis(owners, shuffle, axis=1))


def draw_lengths(key, part):
    drawn = layout(key)
    return drawn[0].astype(jnp.int32)


def draw_assignment(key, part):
    drawn = layout(key)
    return drawn[1].astype(jnp.int32)


def shard_levels(stream_key, dims, split, least, top_value):
    level, own = 1.0, jax.random.fold_in(stream_key, 6)
    for position, shards_of in split:
        heights = jnp.exp(jax.random.uniform(jax.random.fold_in(own, position), (shards_of,), jnp.float32, least / len(split), top_value / len(split)))
        level = level * jnp.repeat(heights, dims[position] // shards_of).reshape([-1 if axis == position else 1 for axis in range(len(dims))])
    return level


def gaussian(own_key, shape, scale, limit, shards=(), held_as=jnp.bfloat16):
    level = shard_levels(own_key, shape, shards, -0.22, 0.18) if shards else 1.0
    values = jax.random.normal(own_key, shape, jnp.float32) * scale * level
    return jnp.minimum(jnp.maximum(values, -limit), limit).astype(held_as)


def setup_inputs(seed: int = 0) -> dict:
    streams_of = jax.random.split(jax.random.key(seed), 13)
    tokens = gaussian(streams_of[0], (MICRO, ROWS, D), 1.0, 6.0, ((1, 16),))
    cotangent = gaussian(streams_of[1], (MICRO, ROWS, D), 1.0, 6.0, ((1, 16),))
    lengths = draw_lengths(jax.random.fold_in(streams_of[12], 71), 0)
    assignment = draw_assignment(jax.random.fold_in(streams_of[12], 71), 0)
    mix_weight = gaussian(streams_of[4], (2, 3, D, D), D ** -0.5, 0.21875, ((0, 2), (2, 4), (3, 4)))
    head_bias = gaussian(streams_of[5], (2, 2, HEADS, HEAD_DIM), 0.5, 3.0, ((0, 2), (2, 4)))
    out_weight = gaussian(streams_of[6], (2, D, D), (D // 64) ** -0.5, 1.75, ((0, 2), (1, 4), (2, 4)))
    norm_gain = jnp.clip(1.0 + 0.15 * jax.random.normal(streams_of[7], (2, 2, D), jnp.float32), 0.25, 1.75).astype(jnp.bfloat16)
    row_shift = gaussian(streams_of[8], (2, 4, D), 0.3, 2.0, ((0, 2),))
    up_weight = gaussian(streams_of[9], (2, D, FF), D ** -0.5, 0.21875, ((0, 2), (1, 4), (2, 4)))
    hidden_bias = gaussian(streams_of[10], (2, FF // 128, 128), 0.5, 3.0, ((0, 2), (1, 4)))
    down_weight = gaussian(streams_of[11], (2, FF, D), FF ** -0.5, 0.109375, ((0, 2), (1, 4), (2, 4)))
    return dict(tokens=tokens, cotangent=cotangent, lengths=lengths, assignment=assignment, mix_weight=mix_weight, head_bias=head_bias, out_weight=out_weight, norm_gain=norm_gain, row_shift=row_shift, up_weight=up_weight, hidden_bias=hidden_bias, down_weight=down_weight)


@jax.custom_vjp
def low(v):
    return lax.optimization_barrier(v.astype(jnp.bfloat16)).astype(jnp.float32)

@jax.custom_vjp
def low_back(v):
    return v

def low_keep(v):
    return (low(v), None)

def low_pass(kept, grad):
    return (grad,)

def back_keep(v):
    return (v, None)

def back_low(kept, grad):
    return (low(grad),)
low.defvjp(low_keep, low_pass)
low_back.defvjp(back_keep, back_low)
EPS = 1e-05
HIGH = lax.Precision.HIGHEST

def product(left, right):
    return jnp.dot(left, right, precision=HIGH)

def layer_norm(values, gain, offset):
    centre = values - lax.optimization_barrier(jnp.mean(values, axis=-1, keepdims=True))
    spread = lax.optimization_barrier(jnp.mean(centre * centre, axis=-1, keepdims=True))
    return centre * lax.rsqrt(spread + EPS) * gain + offset

def segments(lengths, assignment, micro, buffer):
    slots = lengths.shape[1]
    order = jnp.arange(slots, dtype=jnp.int32)
    earlier = (assignment[:, :, None] == assignment[:, None, :]) & (order[None, None, :] < order[None, :, None])
    offset = lax.optimization_barrier(jnp.sum(jnp.where(earlier, lengths[:, None, :], 0), axis=2)).astype(jnp.int32)
    place = jnp.arange(buffer, dtype=jnp.int32)
    batch = jnp.arange(micro, dtype=jnp.int32)
    ending = (offset + lengths).astype(jnp.int32)
    inside = (assignment[:, None, None, :] == batch[None, :, None, None]) & (offset[:, None, None, :] <= place[None, None, :, None]) & (place[None, None, :, None] < ending[:, None, None, :])
    found = lax.optimization_barrier(jnp.sum(jnp.where(inside, order, 0), axis=3)) + jnp.where(jnp.any(inside, axis=3), 0, slots)
    return found.astype(jnp.int32)

def block(hidden, segment, layer):
    mix, head, out, gain, shift, up, inner_bias, down = layer
    count = hidden.shape[0]
    normed = low(layer_norm(hidden, gain[0], shift[0]))
    query = low_back(low(product(normed, mix[0]) + head[0].reshape(-1))).reshape(count, HEADS, HEAD_DIM)
    keys = low_back(low(product(normed, mix[1]))).reshape(count, HEADS, HEAD_DIM)
    values = low_back(low(product(normed, mix[2]) + head[1].reshape(-1))).reshape(count, HEADS, HEAD_DIM)
    scores = low_back(jnp.einsum('qhd,khd->hqk', query, keys, precision=HIGH) * HEAD_DIM ** (-0.5))
    allowed = segment[:, None] == segment[None, :]
    scores = jnp.where(allowed[None], scores, -1e+30)
    lifted = jnp.exp(scores - lax.optimization_barrier(jnp.max(scores, axis=2, keepdims=True)))
    attention = lifted / lax.optimization_barrier(jnp.sum(lifted, axis=2, keepdims=True))
    mixed = jnp.einsum('hqk,khd->qhd', low(attention), values, precision=HIGH).reshape(count, D)
    mixed = low_back(low(mixed))
    after = hidden + low_back(product(mixed, out)) + shift[1]
    normed_two = low(layer_norm(after, gain[1], shift[2]))
    inner = low_back(product(normed_two, up) + inner_bias.reshape(-1))
    activated = low(jax.nn.gelu(inner, approximate=False))
    return after + low_back(product(activated, down)) + shift[3]

def reference(tokens, cotangent, lengths, assignment, mix_weight, head_bias, out_weight, norm_gain, row_shift, up_weight, hidden_bias, down_weight):
    segment = jnp.transpose(segments(lengths, assignment, MICRO, CAP), (1, 0, 2)).reshape(MICRO * GROUPS, CAP)
    live = (segment != SLOTS).astype(jnp.float32)
    inputs = tokens.astype(jnp.float32).reshape(MICRO * GROUPS, CAP, D)
    learned = tuple((item.astype(jnp.float32) for item in (mix_weight, head_bias, out_weight, norm_gain, row_shift, up_weight, hidden_bias, down_weight)))

    def forward(inputs, nudge, learned):

        def one_buffer(item):
            hidden, push, segment_row = item
            first = low(block(hidden, segment_row, tuple((weight[0] for weight in learned))))
            second = low(block(low_back(first + push), segment_row, tuple((weight[1] for weight in learned))))
            return (first, second)
        return lax.map(jax.checkpoint(one_buffer), (inputs, nudge, segment))
    nudge = jnp.zeros_like(inputs)
    outputs, pull = jax.vjp(forward, inputs, nudge, learned)
    start_delta = cotangent.astype(jnp.float32).reshape(MICRO * GROUPS, CAP, D) * live[:, :, None]
    input_part, nudge_part, changes = pull((jnp.zeros_like(outputs[0]), start_delta))
    layer_output = jnp.stack([outputs[0], outputs[1]]).reshape(2, MICRO, GROUPS * CAP, D).astype(jnp.bfloat16)
    input_gradient = jnp.stack([input_part, nudge_part]).reshape(2, MICRO, GROUPS * CAP, D)
    return (layer_output, input_gradient, changes[0], changes[1], changes[2], changes[3], changes[4], changes[5], changes[6], changes[7])
```

```python
from functools import partial

import jax
import jax.numpy as jnp
from jax import lax
from jax.experimental import pallas as pl
from jax.experimental.pallas import tpu as pltpu
from jax.sharding import PartitionSpec as P

HEAD_DIM = 64
EPS = 1e-05
F32 = jnp.float32
BF16 = jnp.bfloat16
SCALE = HEAD_DIM ** (-0.5)
PER_US = 1.1e9
GAIN, SHIFT, HIDDEN, QUERY_BIAS, VALUE_BIAS, PACKED = 0, 2, 6, 7, 8, 16


def shape(dims, dtype):
    return jax.ShapeDtypeStruct(tuple(dims), dtype)


def kernel_call(kernel, outs, *args, scratch=(), smem=0, far=0, mib=16, us=0.5):
    specs = [pl.BlockSpec(memory_space=pltpu.SMEM)] * smem
    specs += [pl.BlockSpec(memory_space=pltpu.VMEM)] * (len(args) - smem - far)
    specs += [pl.BlockSpec(memory_space=pl.ANY)] * far
    return pl.pallas_call(
        kernel,
        out_shape=outs,
        in_specs=specs,
        out_specs=jax.tree.map(lambda _: pl.BlockSpec(memory_space=pltpu.VMEM), outs),
        scratch_shapes=scratch,
        compiler_params=pltpu.CompilerParams(vmem_limit_bytes=mib << 20),
        cost_estimate=pl.CostEstimate(flops=int(us * PER_US), bytes_accessed=1, transcendentals=0),
    )(*args)


def dot(left, right, left_dim, right_dim):
    return lax.dot_general(
        left, right, (((left_dim,), (right_dim,)), ((), ())), preferred_element_type=F32
    )


def nn(left, right):
    return dot(left, right, 1, 0)


def nt(left, right):
    return dot(left, right, 1, 1)


def tn(left, right):
    return dot(left, right, 0, 0)


def normalised(values):
    centre = values - jnp.mean(values, axis=-1, keepdims=True)
    rate = lax.rsqrt(jnp.mean(centre * centre, axis=-1, keepdims=True) + EPS)
    return centre * rate, rate


def head_masks(width):
    lane = lax.broadcasted_iota(jnp.int32, (1, width), 1) // HEAD_DIM
    return [lane == head for head in range(width // HEAD_DIM)]


def only(mask, values):
    return jnp.where(mask, values, jnp.zeros_like(values))


def total_of(parts):
    total = parts[0][...].astype(F32)
    for part in parts[1:]:
        total = total + part[...].astype(F32)
    return total


def pick(core, one, two):
    return jnp.where(core == 0, one, two)


def fetch(sources, held, sems):
    copies = [
        pltpu.make_async_copy(source, target, sems.at[k])
        for k, (source, target) in enumerate(zip(sources, held))
    ]
    for copy in copies:
        copy.start()
    return copies


def enter_kernel(place, lengths, belongs, head, *refs):
    sources, refs = refs[:7], refs[7:]
    entering, pushed, seg_row, vec, inner_own, inner_sent = refs[:6]
    seg_cols, held, sems = refs[6:-8], refs[-8:-1], refs[-1]
    copies = fetch(sources, held, sems)
    tokens, cotangent, gain, shift, hidden, up, down = held
    core, part = place[0], place[2]
    rows, slots, buffer = tokens.shape[1], lengths.shape[1], seg_row.shape[1]
    lane = lax.broadcasted_iota(jnp.int32, (1, buffer), 1)
    row_place = lane
    col_places = []
    for step in range(buffer // rows):
        shifted = ((part ^ step) - step) * rows
        row_place = jnp.where(
            (lane >= step * rows) & (lane < (step + 1) * rows), lane + shifted, row_place
        )
        col_places.append(lax.broadcasted_iota(jnp.int32, (rows, 1), 0) + (part ^ step) * rows)
    places = [row_place] + col_places
    found = [jnp.full(item.shape, slots, jnp.int32) for item in places]
    for slot in range(slots):
        start = jnp.int32(0)
        for other in range(slot):
            start += jnp.where(belongs[0, other] == belongs[0, slot], lengths[0, other], 0)
        stop = jnp.where(belongs[0, slot] == core, start + lengths[0, slot], start)
        found = [
            jnp.where((item >= start) & (item < stop), slot, kept) for item, kept in zip(places, found)
        ]
    seg_row[...] = found[0]
    for out, item in zip(seg_cols, found[1:]):
        out[...] = item
    for copy in copies:
        copy.wait()
    entering[...] = tokens[core]
    push = cotangent[core].astype(F32)
    pushed[...] = jnp.where(found[1] != slots, push, 0.0).astype(BF16)
    vec[...] = jnp.zeros_like(vec)
    vec[GAIN : GAIN + 2] = gain[0].astype(F32)
    vec[SHIFT : SHIFT + 4] = shift[0].astype(F32)
    for item in range(hidden.shape[1]):
        lanes = slice(item * 128, (item + 1) * 128)
        vec[HIDDEN : HIDDEN + 1, lanes] = hidden[0, item : item + 1].astype(F32)
    for kind in range(2):
        row = slice(QUERY_BIAS + kind, QUERY_BIAS + kind + 1)
        vec[row, : head.shape[1]] = head[kind : kind + 1].astype(F32)
    inner_own[...] = pick(core, up[0], down[0])
    inner_sent[...] = pick(core, down[0], up[0])


def pack_kernel(place, *refs):
    sources, (own, sent), held, sems = refs[:2], refs[2:4], refs[4:6], refs[6]
    for copy in fetch(sources, held, sems):
        copy.wait()
    mix, out_weight = held
    core = place[0]
    turned = out_weight[0].T
    cols = turned.shape[1]
    for item, (low, high) in enumerate([(mix[0, 0], mix[0, 2]), (mix[0, 1], turned)]):
        lanes = slice(item * cols, (item + 1) * cols)
        own[:, lanes] = pick(core, low, high)
        sent[:, lanes] = pick(core, high, low)


def pick_kernel(place, one, two, *outs):
    core = place[0]
    outs[0][...] = pick(core, one[...], two[...]).astype(outs[0].dtype)
    outs[1][...] = pick(core, two[...], one[...]).astype(outs[1].dtype)


def place_kernel(place, kept, got, out):
    core = place[0]
    out[0, core] = kept[...].astype(out.dtype)
    out[0, 1 - core] = got[...].astype(out.dtype)


def first_norm_kernel(hidden, vec, normed):
    unit, _ = normalised(hidden[...].astype(F32))
    normed[...] = (unit * vec[GAIN : GAIN + 1] + vec[SHIFT : SHIFT + 1]).astype(BF16)


def project_kernel(normed, mix, vec, query, keys, values):
    width = query.shape[1]
    rows = normed[...]
    query[...] = (nn(rows, mix[0]) + vec[QUERY_BIAS : QUERY_BIAS + 1, :width]).astype(BF16)
    keys[...] = nn(rows, mix[1]).astype(BF16)
    values[...] = (nn(rows, mix[2]) + vec[VALUE_BIAS : VALUE_BIAS + 1, :width]).astype(BF16)


def join_kernel(count, *refs):
    for kind in range(2):
        refs[2 * count + kind][...] = jnp.concatenate(
            [item[...] for item in refs[kind * count : (kind + 1) * count]], axis=0
        )


def attend_kernel(query, keys, values, seg_col, seg_row, mix, partial_out, mixed, weights):
    masks = head_masks(query.shape[1])
    allowed = seg_col[...] == seg_row[...]
    total = None
    for head, mask in enumerate(masks):
        scores = nt(only(mask, query[...]), keys[...]) * SCALE
        scores = jnp.where(allowed, scores, -1e30)
        lifted = jnp.exp(scores - jnp.max(scores, axis=1, keepdims=True))
        attention = (lifted / jnp.sum(lifted, axis=1, keepdims=True)).astype(BF16)
        weights[head] = attention
        part = nn(attention, only(mask, values[...]))
        total = part if total is None else total + part
    rounded = total.astype(BF16)
    mixed[...] = rounded
    partial_out[...] = nt(rounded, mix[3]).astype(partial_out.dtype)


def middle_norm_kernel(count, hidden, vec, *refs):
    parts, after, normed = refs[:count], refs[count], refs[count + 1]
    value = hidden[...].astype(F32) + total_of(parts) + vec[SHIFT + 1 : SHIFT + 2]
    after[...] = value
    unit, _ = normalised(value)
    normed[...] = (unit * vec[GAIN + 1 : GAIN + 2] + vec[SHIFT + 2 : SHIFT + 3]).astype(BF16)


def forward_inner_kernel(normed, pair, vec, partial_out, activated, slope):
    inner = nn(normed[...], pair[0]) + vec[HIDDEN : HIDDEN + 1]
    half = 0.5 + 0.5 * lax.erf(inner * 0.7071067811865476)
    act = (inner * half).astype(BF16)
    activated[...] = act
    slope[...] = half + inner * (jnp.exp(-0.5 * inner * inner) * 0.3989422804014327)
    partial_out[...] = nt(act, pair[1]).astype(partial_out.dtype)


def end_norm_kernel(count, after, vec, next_vec, *refs):
    parts, output = refs[:count], refs[count]
    value = (after[...] + total_of(parts) + vec[SHIFT + 3 : SHIFT + 4]).astype(BF16)
    output[...] = value
    if len(refs) > count + 1:
        unit, _ = normalised(value.astype(F32))
        refs[count + 1][...] = (
            unit * next_vec[GAIN : GAIN + 1] + next_vec[SHIFT : SHIFT + 1]
        ).astype(BF16)


def backward_inner_kernel(delta, pair, slope, partial_out, inner_delta):
    value = (nn(delta[...], pair[1]) * slope[...]).astype(BF16)
    inner_delta[...] = value
    partial_out[...] = nt(value, pair[0]).astype(partial_out.dtype)


def inner_weights_kernel(count, place, *refs):
    normed, inner_delta, delta, activated = (refs[k * count : (k + 1) * count] for k in range(4))
    kept, sent, bias = refs[4 * count :]
    joined = jnp.concatenate([item[...] for item in inner_delta], axis=0)
    bias[...] = jnp.sum(joined.astype(F32), axis=0, keepdims=True)
    core = place[0]
    up = tn(jnp.concatenate([item[...] for item in normed], axis=0), joined).astype(BF16)
    down = tn(
        jnp.concatenate([item[...] for item in delta], axis=0),
        jnp.concatenate([item[...] for item in activated], axis=0),
    ).astype(BF16)
    kept[...] = pick(core, up, down)
    sent[...] = pick(core, down, up)


def norm_pull(delta, values, gain):
    unit, rate = normalised(values)
    scaled = delta * gain
    through = rate * (
        scaled
        - jnp.mean(scaled, axis=-1, keepdims=True)
        - unit * jnp.mean(scaled * unit, axis=-1, keepdims=True)
    )
    return through, jnp.sum(delta * unit, axis=0, keepdims=True), jnp.sum(delta, axis=0, keepdims=True)


def middle_pull_kernel(count, delta_out, after, vec, *refs):
    parts, (full, rounded, sums) = refs[:count], refs[count:]
    delta = delta_out[...].astype(F32)
    through, gain, shift = norm_pull(total_of(parts), after[...], vec[GAIN + 1 : GAIN + 2])
    value = delta + through
    full[...] = value
    rounded[...] = value.astype(BF16)
    sums[0:1] = gain
    sums[1:2] = shift
    sums[2:3] = jnp.sum(value, axis=0, keepdims=True)
    sums[3:4] = jnp.sum(delta, axis=0, keepdims=True)
    sums[4:] = jnp.zeros_like(sums[4:])


def first_pull_kernel(count, after_delta, hidden, vec, *refs):
    parts, (full, sums) = refs[:count], refs[count:]
    through, gain, shift = norm_pull(total_of(parts), hidden[...].astype(F32), vec[GAIN : GAIN + 1])
    full[...] = (after_delta[...] + through).astype(full.dtype)
    sums[0:1] = gain
    sums[1:2] = shift
    sums[2:] = jnp.zeros_like(sums[2:])


def mix_delta_kernel(delta, mix, out):
    out[...] = nn(delta[...], mix[3]).astype(BF16)


def attend_pull_kernel(count, keys, values, *refs):
    query, mix_delta, weights = (refs[k * count : (k + 1) * count] for k in range(3))
    query_delta, keys_delta, values_delta, key_sum, value_sum = refs[3 * count :]
    width = keys.shape[1]
    rows = query[0].shape[0]
    masks = head_masks(width)
    for chunk in range(count):
        query_total, keys_total, values_total = None, None, None
        for head, mask in enumerate(masks):
            rounded = weights[chunk][head]
            attention = rounded.astype(F32)
            delta = only(mask, mix_delta[chunk][...])
            pulled = nt(delta, values[...])
            scored = (
                attention * (pulled - jnp.sum(attention * pulled, axis=1, keepdims=True))
            ).astype(BF16)
            to_query = nn(scored, only(mask, keys[...]))
            to_keys = tn(scored, only(mask, query[chunk][...]))
            to_values = tn(rounded, delta)
            if query_total is None:
                query_total, keys_total, values_total = to_query, to_keys, to_values
            else:
                query_total += to_query
                keys_total += to_keys
                values_total += to_values
        query_delta[chunk] = (query_total * SCALE).astype(BF16)
        if chunk == 0:
            key_sum[...] = keys_total
            value_sum[...] = values_total
        else:
            key_sum[...] += keys_total
            value_sum[...] += values_total
    for chunk in range(count):
        part = slice(chunk * rows, (chunk + 1) * rows)
        keys_delta[chunk] = (key_sum[part] * SCALE).astype(BF16)
        values_delta[chunk] = value_sum[part].astype(BF16)


def project_pull_kernel(chunk, query_delta, keys_delta, values_delta, mix, partial_out):
    total = nt(query_delta[chunk], mix[0])
    total += nt(keys_delta[chunk], mix[1])
    total += nt(values_delta[chunk], mix[2])
    partial_out[...] = total.astype(partial_out.dtype)


def mix_weights_kernel(count, place, query_delta, keys_delta, values_delta, *refs):
    normed, delta, mixed = (refs[k * count : (k + 1) * count] for k in range(3))
    kept, sent, bias = refs[3 * count :]

    def joined(item):
        return jnp.concatenate([item[k] for k in range(count)], axis=0)

    core = place[0]
    rows = jnp.concatenate([item[...] for item in normed], axis=0)
    by_query, by_keys, by_values = joined(query_delta), joined(keys_delta), joined(values_delta)
    of_query, of_keys = tn(rows, by_query).astype(BF16), tn(rows, by_keys).astype(BF16)
    of_values = tn(rows, by_values).astype(BF16)
    of_out = tn(
        jnp.concatenate([item[...] for item in delta], axis=0),
        jnp.concatenate([item[...] for item in mixed], axis=0),
    ).astype(BF16)
    cols = of_out.shape[1]
    for item, (low, high) in enumerate([(of_query, of_values), (of_keys, of_out)]):
        lanes = slice(item * cols, (item + 1) * cols)
        kept[:, lanes] = pick(core, low, high)
        sent[:, lanes] = pick(core, high, low)
    bias[0:1] = jnp.sum(by_query.astype(F32), axis=0, keepdims=True)
    bias[1:2] = jnp.sum(by_values.astype(F32), axis=0, keepdims=True)


def sums_kernel(place, *refs):
    layers, (kept, sent) = (refs[:4], refs[4:8]), refs[8:]
    core = place[0]
    kept[...] = jnp.zeros_like(kept)
    sent[...] = jnp.zeros_like(sent)

    def put(row, lanes, values):
        kept[row : row + 1, :lanes] = pick(core, values[0], values[1])
        sent[row : row + 1, :lanes] = pick(core, values[1], values[0])

    width = kept.shape[1]
    for row, source, at in ((0, 0, 0), (1, 1, 0), (2, 0, 1), (3, 1, 2), (4, 1, 1), (5, 1, 3)):
        put(row, width, [layer[source][at : at + 1] for layer in layers])
    put(6, layers[0][2].shape[1], [layer[2][...] for layer in layers])
    for kind in range(2):
        put(7 + kind, layers[0][3].shape[1], [layer[3][kind : kind + 1] for layer in layers])


def pieces_kernel(ways, wide, fine, place, kept, received, pieces):
    part = place[2]
    sums = kept[...] + received[...]
    peers = pieces.shape[0] // ways
    pieces[...] = jnp.zeros_like(pieces)
    for owner in range(ways * peers):
        group = owner // peers
        here = part == owner % peers
        pieces[owner, :6, :wide] = sums[:6, owner * wide : (owner + 1) * wide]
        for item in range(sums.shape[1] // 128):
            start = item * 128 + group * (128 // ways)
            pieces[owner, 8 + item : 9 + item, : 128 // ways] = jnp.where(
                here, sums[6:7, start : start + 128 // ways], 0.0
            )
        for item in range(fine):
            start = item * HEAD_DIM + group * (HEAD_DIM // ways)
            for kind in range(2):
                row = kind * fine + item
                pieces[owner, row : row + 1, 64 : 64 + HEAD_DIM // ways] = jnp.where(
                    here, sums[7 + kind : 8 + kind, start : start + HEAD_DIM // ways], 0.0
                )


def assemble_kernel(part, place, *refs):
    ways, out = len(refs) - 1, refs[-1]
    for step in range(ways):
        owner = lax.rem(place[1] - step + ways, ways)
        out[pl.ds(pl.multiple_of(owner * part, part), part), :] = refs[step][...]


def unpack_kernel(place, own, other, out):
    core = place[0]
    cols = out.shape[2]
    each = out.shape[0] // 2
    for item in range(each):
        lanes = slice(item * cols, (item + 1) * cols)
        out[item] = pick(core, own[:, lanes], other[:, lanes])
        out[each + item] = pick(core, other[:, lanes], own[:, lanes])


def presum_kernel(kept, received, out):
    out[...] = (kept[...].astype(F32) + received[...].astype(F32)).astype(out.dtype)


def presum_shards_kernel(part, place, kept, received, *outs):
    ways = len(outs)
    for step in range(ways):
        owner = lax.rem(place[1] + step, ways)
        rows = pl.ds(pl.multiple_of(owner * part, part), part)
        outs[step][...] = (
            kept[rows, :].astype(F32) + received[rows, :].astype(F32)
        ).astype(outs[step].dtype)


def final_sum_kernel(*refs):
    refs[-1][...] = total_of(refs[:-1])


def inner_out_kernel(place, kept, got, up, down):
    core = place[0]
    up[0] = pick(core, kept[...], got[...]).astype(F32)
    down[0] = pick(core, got[...], kept[...]).astype(F32)


def mix_out_kernel(place, kept, got, mix, out):
    core = place[0]
    cols = mix.shape[3]
    low = pick(core, kept[...], got[...]).astype(F32)
    high = pick(core, got[...], kept[...]).astype(F32)
    mix[0, 0] = low[:, :cols]
    mix[0, 1] = low[:, cols:]
    mix[0, 2] = high[:, :cols]
    out[0] = high[:, cols:].T


def shares_kernel(pieces, gain, shift, hidden, head):
    total = pieces[0]
    for owner in range(1, pieces.shape[0]):
        total += pieces[owner]
    gain[0] = total[:2, : gain.shape[2]]
    shift[0] = total[2:6, : shift.shape[2]]
    hidden[0] = total[8 : 8 + hidden.shape[1], : hidden.shape[2]]
    fine, each = head.shape[2:]
    for kind in range(2):
        head[0, kind] = total[kind * fine : (kind + 1) * fine, 64 : 64 + each]


def after(value, *others):
    if not others:
        return value
    return lax.optimization_barrier((value,) + others)[0]


def other_core(value):
    return lax.ppermute(value, "section", [(0, 1), (1, 0)])


def to_peer(value, mask, count):
    return lax.ppermute(value, "tensor", [(k, k ^ mask) for k in range(count)])


def along(value, steps, ways):
    return lax.ppermute(value, "dp", [(k, (k + steps) % ways) for k in range(ways)])


def on_device(
    tokens,
    cotangent,
    lengths,
    assignment,
    mix_weight,
    head_bias,
    out_weight,
    norm_gain,
    row_shift,
    up_weight,
    hidden_bias,
    down_weight,
):
    peers = lax.axis_size("tensor")
    ways = lax.axis_size("dp")
    micro, rows, width = tokens.shape
    buffer = rows * peers
    heads_width = out_weight.shape[1]
    heads = heads_width // HEAD_DIM
    units = up_weight.shape[2]
    shard = width // ways
    stepped = shard % 16 == 0
    order = [3, 1, 2][: peers - 1] if peers == 4 else list(range(1, peers))
    place = jnp.stack([lax.axis_index(axis) for axis in ("section", "dp", "tensor")]).astype(jnp.int32)
    given = (
        place,
        tokens,
        cotangent,
        lengths,
        assignment,
        mix_weight,
        out_weight,
        up_weight,
        jnp.swapaxes(down_weight, 1, 2),
        norm_gain,
        row_shift,
        hidden_bias,
        head_bias.reshape(2, heads_width),
    )
    place, tokens, cotangent, lengths, assignment, mix_weight, out_weight = (
        given := lax.optimization_barrier(given)
    )[:7]
    up_weight, turned_down, norm_gain, row_shift, hidden_bias, flat_head = given[7:]

    latest = []

    def run(kernel, outs, *args, smem=0, **options):
        args = list(args)
        if latest:
            args[smem] = after(args[smem], latest[-1])
        done = kernel_call(kernel, outs, *args, smem=smem, **options)
        latest[:] = [jax.tree.leaves(done)[0]]
        return done

    def placed(kernel, outs, *args, **options):
        return run(kernel, outs, place, *args, smem=1, **options)

    def scratch_of(*items):
        return [pltpu.VMEM(item.shape, item.dtype) for item in items] + [
            pltpu.SemaphoreType.DMA((len(items),))
        ]

    def picked(one, two, *types):
        return placed(pick_kernel, [shape(one.shape, item) for item in types], one, two, mib=8)

    def collect(chunk):
        got = {step: to_peer(chunk, step, peers) for step in order}
        return [chunk] + [got[step] for step in range(1, peers)]

    def spread(parts):
        got = {step: to_peer(parts[step], step, peers) for step in order}
        return [parts[0]] + [got[step] for step in range(1, peers)]

    def part_type(step):
        return F32 if step == 0 else BF16

    def gather(half, *before, chained=True):
        half = after(half, *before)
        if not stepped:
            return [lax.all_gather(half, "dp", axis=0, tiled=True)]
        held = [half]
        for step in range(1, ways):
            held.append(along(after(half, held[-1]) if chained and step > 1 else half, step, ways))
        return held

    def assembled(held, *before):
        held = [after(held[0], *before)] + held[1:]
        own = held[0]
        if stepped:
            own = placed(partial(assemble_kernel, shard), shape((width, own.shape[1]), BF16), *held, mib=4)
        return own

    def unpacked(own, items, *before):
        other = other_core(after(own, *before))
        out = shape((2 * items, width, own.shape[1] // items), BF16)
        return placed(unpack_kernel, out, own, other, mib=8)

    def project(chunk, mix, vec):
        return run(
            project_kernel,
            [shape((rows, heads_width), BF16)] * 3,
            chunk,
            mix,
            vec,
            mib=4,
            us=0.4,
        )

    def join(projected):
        return run(
            partial(join_kernel, peers),
            [shape((buffer, heads_width), BF16)] * 2,
            *[item[1] for item in projected],
            *[item[2] for item in projected],
            mib=4,
        )

    def attend(step, query, keys, values, mix):
        return run(
            attend_kernel,
            [
                shape((rows, width), part_type(step)),
                shape((rows, heads_width), BF16),
                shape((heads, rows, buffer), BF16),
            ],
            query,
            keys,
            values,
            seg_cols[step],
            seg_row,
            mix,
            mib=8,
            us=1.5,
        )

    def attention(whole, vec, mix, at_join=(), at_third=(), at_last=()):
        projected = {step: project(whole[step], mix, vec) for step in [0] + order}
        projected = [projected[step] for step in range(peers)]
        if at_join:
            projected[0] = (projected[0][0], after(projected[0][1], *at_join), projected[0][2])
        keys, values = join(projected)
        pins = {(order + [0])[2 % peers]: at_third, 0: at_last}
        attended = {
            step: attend(step, after(projected[step][0], *pins.get(step, ())), keys, values, mix)
            for step in order + [0]
        }
        attended = [attended[step] for step in range(peers)]
        query, mixed = [item[0] for item in projected], [item[1] for item in attended]
        kept = (query, keys, values, [item[2] for item in attended], mixed)
        return spread([item[0] for item in attended]), kept

    def middle_norm(hidden, vec, parts):
        return run(
            partial(middle_norm_kernel, peers),
            [shape((rows, width), F32), shape((rows, width), BF16)],
            hidden,
            vec,
            *parts,
            mib=4,
        )

    def forward_inner(step, normed, pair, vec):
        return run(
            forward_inner_kernel,
            [
                shape((rows, width), part_type(step)),
                shape((rows, units), BF16),
                shape((rows, units), F32),
            ],
            normed,
            pair,
            vec,
            mib=8,
            us=0.8,
        )

    def end_norm(after_rows, vec, next_vec, parts):
        return run(
            partial(end_norm_kernel, peers),
            [shape((rows, width), BF16)] * (1 if next_vec is None else 2),
            after_rows,
            vec,
            vec if next_vec is None else next_vec,
            *parts,
            mib=4,
        )

    def backward_inner(step, delta, pair, slope):
        return run(
            backward_inner_kernel,
            [shape((rows, width), part_type(step)), shape((rows, units), BF16)],
            delta,
            pair,
            slope,
            mib=8,
            us=0.8,
        )

    def inner_weights(normed, inner_delta, delta, activated):
        return placed(
            partial(inner_weights_kernel, peers),
            [shape((width, units), BF16)] * 2 + [shape((1, units), F32)],
            *normed,
            *inner_delta,
            *delta,
            *activated,
            mib=16,
            us=2.6,
        )

    def middle_pull(delta, after_rows, vec, parts):
        return run(
            partial(middle_pull_kernel, peers),
            [shape((rows, width), F32), shape((rows, width), BF16), shape((8, width), F32)],
            delta,
            after_rows,
            vec,
            *parts,
            mib=8,
        )

    def attention_delta(whole_after, mix):
        mix_delta = {
            step: run(
                mix_delta_kernel,
                shape((rows, heads_width), BF16),
                whole_after[step],
                mix,
                mib=4,
                us=0.3,
            )
            for step in [0] + order
        }
        return [mix_delta[step] for step in range(peers)]

    def attention_pull(mix_delta, kept, mix, before):
        query, keys, values, weights, _ = kept
        three = run(
            partial(attend_pull_kernel, peers),
            [shape((peers, rows, heads_width), BF16)] * 3,
            after(keys, *before),
            values,
            *query,
            *mix_delta,
            *weights,
            scratch=[pltpu.VMEM((buffer, heads_width), F32)] * 2,
            mib=16,
            us=6.6,
        )
        parts = {
            step: run(
                partial(project_pull_kernel, step),
                shape((rows, width), part_type(step)),
                *three,
                mix,
                mib=4,
                us=0.55,
            )
            for step in order + [0]
        }
        return three, spread([parts[step] for step in range(peers)])

    def mix_weights(three, whole, whole_after, mixed):
        return placed(
            partial(mix_weights_kernel, peers),
            [shape((width, 2 * heads_width), BF16)] * 2 + [shape((2, heads_width), F32)],
            *three,
            *whole,
            *whole_after,
            *mixed,
            mib=16,
            us=2.1,
        )

    def first_pull(after_delta, hidden, vec, parts, dtype):
        return run(
            partial(first_pull_kernel, peers),
            [shape((rows, width), dtype), shape((8, width), F32)],
            after_delta,
            hidden,
            vec,
            *parts,
            mib=8,
        )

    def presummed(kept, got):
        cols = got.shape[1]
        if not stepped:
            both = run(presum_kernel, shape(got.shape, BF16), kept, got, mib=4)
            return [lax.psum_scatter(both, "dp", scatter_dimension=0, tiled=True)]
        chunks = placed(
            partial(presum_shards_kernel, shard),
            [shape((shard, cols), F32 if step == 0 else BF16) for step in range(ways)],
            kept,
            got,
            mib=4,
        )
        return [chunks[0]] + [along(chunks[step], step, ways) for step in range(1, ways)]

    def settled(parts):
        if not stepped:
            return parts[0].astype(F32)
        return run(final_sum_kernel, shape(parts[0].shape, F32), *parts, mib=4)

    sources = (mix_weight, out_weight)
    mix_own, mix_sent = placed(
        pack_kernel,
        [shape((shard, 2 * heads_width), BF16)] * 2,
        *sources,
        scratch=scratch_of(*sources),
        far=2,
        mib=8,
    )
    mix_got = other_core(mix_sent)
    sources = (tokens, cotangent, norm_gain, row_shift, hidden_bias, up_weight, turned_down)
    entered = run(
        enter_kernel,
        [shape((rows, width), BF16)] * 2
        + [shape((1, buffer), jnp.int32), shape((PACKED, width), F32)]
        + [shape((shard, units), BF16)] * 2
        + [shape((rows, 1), jnp.int32)] * peers,
        place,
        lengths,
        assignment,
        flat_head,
        *sources,
        scratch=scratch_of(*sources),
        smem=3,
        far=7,
        mib=8,
    )
    entering, pushed, seg_row, vec_own, inner_own, inner_sent = entered[:6]
    seg_cols = entered[6:]
    vec_got, inner_got = other_core(vec_own), other_core(inner_sent)
    mix_halves = picked(mix_own, mix_got, BF16, BF16)
    held_mix_one = gather(mix_halves[0], chained=False)
    vecs = picked(vec_own, vec_got, F32, F32)
    normed = run(first_norm_kernel, shape((rows, width), BF16), entering, vecs[0], mib=4)
    whole_one = collect(normed)
    inner_halves = picked(inner_own, inner_got, BF16, BF16)
    held_inner_one = gather(inner_halves[0], *held_mix_one)
    whole_push = collect(after(pushed, *whole_one))
    held_mix_two = gather(mix_halves[1], *held_inner_one)
    held_inner_two = gather(inner_halves[1], *held_mix_two)

    mix_one = unpacked(assembled(held_mix_one, *whole_one), 2)
    parts, kept_one = attention(
        whole_one,
        vecs[0],
        mix_one,
        at_join=held_inner_one[1:2],
        at_third=whole_push[1:],
        at_last=held_inner_one[2:3],
    )
    after_one, normed = middle_norm(entering, vecs[0], parts)
    whole_inner_one = collect(normed)
    pair_one = unpacked(assembled(held_inner_one), 1)
    whole_inner_one[order[0]] = after(whole_inner_one[order[0]], *held_mix_two[1:2])
    whole_inner_one[order[-1]] = after(whole_inner_one[order[-1]], *held_mix_two[2:3])
    inner_one = {
        step: forward_inner(step, whole_inner_one[step], pair_one, vecs[0]) for step in [0] + order
    }
    parts = spread([inner_one[step][0] for step in range(peers)])
    mix_two = assembled(held_mix_two)
    output_one, normed = end_norm(after_one, vecs[0], vecs[1], parts)
    whole_two = collect(normed)

    mix_two = unpacked(mix_two, 2, output_one)
    parts, kept_two = attention(
        whole_two,
        vecs[1],
        mix_two,
        at_join=held_inner_two[1:2],
        at_last=held_inner_two[2:3],
    )
    after_two, normed = middle_norm(output_one, vecs[1], parts)
    whole_inner_two = collect(normed)
    pair_two = unpacked(assembled(held_inner_two), 1)
    inner_two, pulled = {}, {}
    for step in [0] + order:
        inner_two[step] = forward_inner(step, whole_inner_two[step], pair_two, vecs[1])
        pulled[step] = backward_inner(step, whole_push[step], pair_two, inner_two[step][2])
    parts = spread([pulled[step][0] for step in range(peers)])
    inner_kept, inner_given, hidden_sum = inner_weights(
        whole_inner_two,
        [pulled[step][1] for step in range(peers)],
        whole_push,
        [inner_two[step][1] for step in range(peers)],
    )
    after_delta, rounded, sums_middle = middle_pull(pushed, after_two, vecs[1], parts)
    whole_after = collect(rounded)
    inner_got = other_core(after(inner_given, rounded))
    mix_delta = attention_delta(whole_after, mix_two)
    inner_parts_two = presummed(inner_kept, inner_got)
    three, parts = attention_pull(mix_delta, kept_two, mix_two, inner_parts_two[1:2])
    mix_kept, mix_given, head_sum = mix_weights(three, whole_two, whole_after, kept_two[4])
    delta_two, sums_first = first_pull(
        after(after_delta, *inner_parts_two[2:3]), output_one, vecs[1], parts, BF16
    )
    vectors_two = (sums_first, sums_middle, hidden_sum, head_sum)
    whole_delta = collect(delta_two)
    mix_got = other_core(after(mix_given, delta_two))

    pulled = {0: backward_inner(0, whole_delta[0], pair_one, inner_one[0][2])}
    mix_parts_two = presummed(mix_kept, mix_got)
    whole_delta[order[-1]] = after(whole_delta[order[-1]], *inner_parts_two[3:])
    for step in order:
        pulled[step] = backward_inner(step, whole_delta[step], pair_one, inner_one[step][2])
    parts = spread([pulled[step][0] for step in range(peers)])
    inner_kept, inner_given, hidden_sum = inner_weights(
        whole_inner_one,
        [pulled[step][1] for step in range(peers)],
        whole_delta,
        [inner_one[step][1] for step in range(peers)],
    )
    inner_total_two = settled(inner_parts_two)
    after_delta, rounded, sums_middle = middle_pull(
        after(delta_two, *mix_parts_two[1:2]), after_one, vecs[0], parts
    )
    whole_after = collect(rounded)
    inner_got = other_core(after(inner_given, rounded))
    mix_delta = attention_delta(whole_after, mix_one)
    inner_parts_one = presummed(inner_kept, inner_got)
    late = [after(inner_two[step][0], *whole_after) for step in range(peers)]
    late = spread(late)
    three, parts = attention_pull(mix_delta, kept_one, mix_one, mix_parts_two[2:])
    mix_kept, mix_given, head_sum = mix_weights(three, whole_one, whole_after, kept_one[4])
    mix_total_two = settled(mix_parts_two)
    (output_two,) = end_norm(after_two, vecs[1], None, late)
    output_kept, output_given = picked(output_one, output_two, BF16, BF16)
    delta_one, sums_first = first_pull(
        after(after_delta, *inner_parts_one[1:2]), entering, vecs[0], parts, F32
    )
    mix_got = other_core(after(mix_given, sums_first))
    output_got = other_core(after(output_given, sums_first))
    vectors_one = (sums_first, sums_middle, hidden_sum, head_sum)

    sums_kept, sums_given = placed(
        sums_kernel, [shape((PACKED, width), F32)] * 2, *vectors_one, *vectors_two, mib=4
    )
    sums_got = other_core(sums_given)
    mix_parts_one = presummed(mix_kept, mix_got)
    delta_kept, delta_given = picked(delta_one, delta_two, F32, F32)
    delta_got = other_core(delta_given)
    pieces = placed(
        partial(pieces_kernel, ways, width // (ways * peers), heads),
        shape((ways * peers, 16, 128), F32),
        sums_kept,
        sums_got,
        mib=4,
    )
    pieces = lax.all_to_all(pieces, ("dp", "tensor"), 0, 0, tiled=True)

    def by_core(kept, got):
        return placed(place_kernel, shape((1, 2) + kept.shape, kept.dtype), kept, got, mib=8)

    layer_output = by_core(output_kept, output_got)
    inner_kept, inner_given = picked(settled(inner_parts_one), inner_total_two, F32, F32)
    inner_got = other_core(inner_given)
    input_gradient = by_core(delta_kept, delta_got)
    up_gradient, down_gradient = placed(
        inner_out_kernel, [shape((1, shard, units), F32)] * 2, inner_kept, inner_got, mib=4
    )
    mix_kept, mix_given = picked(settled(mix_parts_one), mix_total_two, F32, F32)
    mix_gradient, out_gradient = placed(
        mix_out_kernel,
        [shape((1, 3, shard, heads_width), F32), shape((1, heads_width, shard), F32)],
        mix_kept,
        other_core(mix_given),
        mib=4,
    )
    gain_gradient, shift_gradient, hidden_gradient, head_gradient = run(
        shares_kernel,
        [
            shape((1, 2, width // (ways * peers)), F32),
            shape((1, 4, width // (ways * peers)), F32),
            shape((1, units // 128, 128 // ways), F32),
            shape((1, 2, heads, HEAD_DIM // ways), F32),
        ],
        pieces,
        mib=4,
    )
    return (
        layer_output,
        input_gradient,
        mix_gradient,
        head_gradient,
        out_gradient,
        gain_gradient,
        shift_gradient,
        up_gradient,
        hidden_gradient,
        jnp.swapaxes(down_gradient, 1, 2),
    )


def solution(mesh):
    placed = (
        P(None, ("dp", "tensor"), None),
        P(None, ("dp", "tensor"), None),
        P("dp", None),
        P("dp", None),
        P("section", None, "dp", "tensor"),
        P("section", None, "tensor", None),
        P("section", "tensor", "dp"),
        P("section", None, None),
        P("section", None, None),
        P("section", "dp", "tensor"),
        P("section", "tensor", None),
        P("section", "tensor", "dp"),
    )
    return jax.shard_map(
        on_device,
        mesh=mesh,
        in_specs=placed,
        out_specs=(
            P("section", None, ("dp", "tensor"), None),
            P("section", None, ("dp", "tensor"), None),
            P("section", None, "dp", "tensor"),
            P("section", None, "tensor", "dp"),
            P("section", "tensor", "dp"),
            P("section", None, ("dp", "tensor")),
            P("section", None, ("dp", "tensor")),
            P("section", "dp", "tensor"),
            P("section", "tensor", "dp"),
            P("section", "tensor", "dp"),
        ),
        check_vma=False,
    )
```

```python
from functools import partial

import jax
import jax.numpy as jnp
from jax import lax
from jax.experimental import pallas as pl
from jax.experimental.pallas import tpu as pltpu
from jax.sharding import PartitionSpec as P

HEAD_DIM = 64
EPS = 1e-05
F32 = jnp.float32
BF16 = jnp.bfloat16
SCALE = HEAD_DIM ** (-0.5)
PER_US = 1.1e9
COSTS = dict(
    other=0.5,
    project=0.12,
    attend=1.5,
    forward_inner=1.6,
    backward_inner=0.8,
    inner_weights=7.8,
    mix_delta=0.9,
    attend_pull=2.3,
    project_pull=0.405,
    mix_weights=2.1,
    stack=0.45,
    middle_norm=0.525,
    end_norm=1.5,
    middle_pull=0.5,
    first_pull=1.5,
    presum_shards=0.75,
    halfway=0.5,
    final_sum=0.25,
    join=0.5,
    unpack=0.8,
    assemble=0.5,
    first_norm=0.075,
    enter=6.0,
)
SWITCHES = dict(
    first=3,
    order=[2, 1, 3],
    take=[2, 1, 3],
    give=[2, 1, 3],
)
PLACES = dict(
    inner1_far=0.0,
    inner1_stack=5.0,
    inner1_join=10.0,
    inner1=13.5,
    push=5.0,
    mix2_far=10.0,
    mix2_stack=13.0,
    mix2_join=22.0,
    mix2=29.5,
    inner2_far=9.2,
    inner2_stack=22.0,
    inner2_join=25.0,
    inner2=25.5,
    d_inner2_given=34.0,
    d_inner2_sum=34.8,
    d_inner2_half=41.0,
    d_inner2=50.0,
    late=45.8,
    late_end=52.0,
    late_given=50.842,
    d_mix2_given=40.0,
    d_mix2_sum=41.0,
    d_mix2_half=44.0,
    d_mix2=52.148,
    d_inner1_given=45.0,
    d_inner1_sum=45.8,
    d_inner1_half=50.68,
    d_inner1=52.014,
    d_mix1_given=48.8,
    d_mix1_sum=51.1,
    d_mix1_half=51.5,
    d_mix1=51.722,
    sums=51.569,
    delta=47.945,
    pieces=51.45,
    shares=51.85,
    delta_out=51.6,
    late_out=51.65,
    inner_given=51.41,
    inner_out=51.7,
    mix_given=51.85,
    mix_out=52.129,
    out1=0.2,
    out2=16.6,
    after2=34.0,
    after1=42.0,
    out1_held=6,
    out2_held=22.0,
    d_mix2_half_held=44.6,
    d_mix1_half_held=51.209,
    d_mix2_sum_held=45.0,
    push_held=8.0,
    d_inner1_half_held=51.68,
    mix2_far_held=18.0,
    inner1_far_held=5.0,
    d_inner2_parts=33,
    d_mix2_parts=39,
    d_inner1_parts=45,
    d_mix1_parts=49,
    d_inner2_half_held=49.0,
)
GAIN, SHIFT, HIDDEN, QUERY_BIAS, VALUE_BIAS, PACKED = 0, 2, 6, 7, 8, 16


def name_of(kernel):
    return getattr(kernel, "func", kernel).__name__[: -len("_kernel")]


def shape(dims, dtype):
    return jax.ShapeDtypeStruct(tuple(dims), dtype)


def kernel_call(kernel, outs, *args, scratch=(), smem=0, far=0, mib=16):
    near = len(args) - far
    args = args[:near] + tuple(pltpu.with_memory_space_constraint(item, pltpu.HBM) for item in args[near:])
    specs = [pl.BlockSpec(memory_space=pltpu.SMEM)] * smem
    specs += [pl.BlockSpec(memory_space=pltpu.VMEM)] * (len(args) - smem - far)
    specs += [pl.BlockSpec(memory_space=pltpu.HBM)] * far
    return pl.pallas_call(
        kernel,
        name='K_'+name_of(kernel),
        out_shape=outs,
        in_specs=specs,
        out_specs=jax.tree.map(lambda _: pl.BlockSpec(memory_space=pltpu.VMEM), outs),
        scratch_shapes=scratch,
        compiler_params=pltpu.CompilerParams(vmem_limit_bytes=mib << 20),
        cost_estimate=pl.CostEstimate(flops=int(COSTS.get(name_of(kernel), COSTS['other']) * PER_US), bytes_accessed=1, transcendentals=0),
    )(*args)


def dot(left, right, left_dim, right_dim):
    return lax.dot_general(
        left, right, (((left_dim,), (right_dim,)), ((), ())), preferred_element_type=F32
    )


def nn(left, right):
    return dot(left, right, 1, 0)


def nt(left, right):
    return dot(left, right, 1, 1)


def tn(left, right):
    return dot(left, right, 0, 0)


def normalised(values):
    centre = values - jnp.mean(values, axis=-1, keepdims=True)
    rate = lax.rsqrt(jnp.mean(centre * centre, axis=-1, keepdims=True) + EPS)
    return centre * rate, rate


def head_masks(width):
    lane = lax.broadcasted_iota(jnp.int32, (1, width), 1) // HEAD_DIM
    return [lane == head for head in range(width // HEAD_DIM)]


def only(mask, values):
    return jnp.where(mask, values, jnp.zeros_like(values))


def total_of(parts):
    total = parts[0][...].astype(F32)
    for part in parts[1:]:
        total = total + part[...].astype(F32)
    return total


def pick(core, one, two):
    return jnp.where(core == 0, one, two)


def fetch(sources, held, sems):
    copies = [
        pltpu.make_async_copy(source, target, sems.at[k])
        for k, (source, target) in enumerate(zip(sources, held))
    ]
    for copy in copies:
        copy.start()
    return copies


def enter_kernel(place, lengths, belongs, head, *refs):
    sources, refs = refs[:7], refs[7:]
    entering, pushed, seg_row, vec, inner_own, inner_sent = refs[:6]
    seg_cols, held, sems = refs[6:-8], refs[-8:-1], refs[-1]
    copies = fetch(sources, held, sems)
    tokens, cotangent, gain, shift, hidden, up, down = held
    core, part = place[0], place[2]
    rows, slots, buffer = tokens.shape[1], lengths.shape[1], seg_row.shape[1]
    lane = lax.broadcasted_iota(jnp.int32, (1, buffer), 1)
    row_place = lane
    col_places = []
    for step in range(buffer // rows):
        shifted = ((part ^ step) - step) * rows
        row_place = jnp.where(
            (lane >= step * rows) & (lane < (step + 1) * rows), lane + shifted, row_place
        )
        col_places.append(lax.broadcasted_iota(jnp.int32, (rows, 1), 0) + (part ^ step) * rows)
    places = [row_place] + col_places
    found = [jnp.full(item.shape, slots, jnp.int32) for item in places]
    for slot in range(slots):
        start = jnp.int32(0)
        for other in range(slot):
            start += jnp.where(belongs[0, other] == belongs[0, slot], lengths[0, other], 0)
        stop = jnp.where(belongs[0, slot] == core, start + lengths[0, slot], start)
        found = [
            jnp.where((item >= start) & (item < stop), slot, kept) for item, kept in zip(places, found)
        ]
    seg_row[...] = found[0]
    for out, item in zip(seg_cols, found[1:]):
        out[...] = item
    for copy in copies:
        copy.wait()
    entering[...] = tokens[core]
    push = cotangent[core].astype(F32)
    pushed[...] = jnp.where(found[1] != slots, push, 0.0).astype(BF16)
    vec[...] = jnp.zeros_like(vec)
    vec[GAIN : GAIN + 2] = gain[0].astype(F32)
    vec[SHIFT : SHIFT + 4] = shift[0].astype(F32)
    for item in range(hidden.shape[1]):
        lanes = slice(item * 128, (item + 1) * 128)
        vec[HIDDEN : HIDDEN + 1, lanes] = hidden[0, item : item + 1].astype(F32)
    for item in range(head.shape[1]):
        lanes = slice(item * HEAD_DIM, (item + 1) * HEAD_DIM)
        vec[QUERY_BIAS : QUERY_BIAS + 2, lanes] = head[0, item].astype(F32)
    inner_own[...] = pick(core, up[0], down[0])
    inner_sent[...] = pick(core, down[0], up[0])


def pack_kernel(place, *refs):
    sources, (own, sent), held, sems = refs[:2], refs[2:4], refs[4:6], refs[6]
    for copy in fetch(sources, held, sems):
        copy.wait()
    mix, out_weight = held
    core = place[0]
    turned = out_weight[0].T
    cols = turned.shape[1]
    for item, (low, high) in enumerate([(mix[0, 0], mix[0, 2]), (mix[0, 1], turned)]):
        lanes = slice(item * cols, (item + 1) * cols)
        own[:, lanes] = pick(core, low, high)
        sent[:, lanes] = pick(core, high, low)


def pick_kernel(place, one, two, *outs):
    core = place[0]
    outs[0][...] = pick(core, one[...], two[...]).astype(outs[0].dtype)
    outs[1][...] = pick(core, two[...], one[...]).astype(outs[1].dtype)


def place_kernel(place, kept, got, out):
    core = place[0]
    out[0, core] = kept[...].astype(out.dtype)
    out[0, 1 - core] = got[...].astype(out.dtype)


def first_norm_kernel(hidden, vec, normed):
    unit, _ = normalised(hidden[...].astype(F32))
    normed[...] = (unit * vec[GAIN : GAIN + 1] + vec[SHIFT : SHIFT + 1]).astype(BF16)


def project_kernel(normed, mix, vec, query, keys, values):
    width = query.shape[1]
    rows = normed[...]
    query[...] = (nn(rows, mix[0]) + vec[QUERY_BIAS : QUERY_BIAS + 1, :width]).astype(BF16)
    keys[...] = nn(rows, mix[1]).astype(BF16)
    values[...] = (nn(rows, mix[2]) + vec[VALUE_BIAS : VALUE_BIAS + 1, :width]).astype(BF16)


def join_kernel(count, *refs):
    for kind in range(2):
        refs[2 * count + kind][...] = jnp.concatenate(
            [item[...] for item in refs[kind * count : (kind + 1) * count]], axis=0
        )


def attend_kernel(query, keys, values, seg_col, seg_row, mixed, rounded, weights):
    masks = head_masks(query.shape[1])
    barred = jnp.where(seg_col[...] == seg_row[...], 0.0, -1e30)
    scaled = query[...] * jnp.asarray(SCALE, BF16)
    total = None
    for head, mask in enumerate(masks):
        scores = nt(only(mask, scaled), keys[...]) + barred
        lifted = jnp.exp(scores - jnp.max(scores, axis=1, keepdims=True))
        attention = (lifted * (1.0 / jnp.sum(lifted, axis=1, keepdims=True))).astype(BF16)
        weights[head] = attention
        part = nn(attention, only(mask, values[...]))
        total = part if total is None else total + part
    mixed[...] = total
    rounded[...] = total.astype(BF16)


def middle_norm_kernel(count, place, hidden, vec, *refs):
    mixed, outs, (after, normed) = refs[:count], refs[count : 3 * count], refs[3 * count :]
    mine = sum(nt(part[...], out[...]) for part, out in zip(mixed, outs[:count]))
    other = sum(nt(part[...], out[...]) for part, out in zip(mixed, outs[count:]))
    core = place[0]
    value = jnp.concatenate([pick(core, mine, other), pick(core, other, mine)], axis=1)
    value = value + hidden[...].astype(F32) + vec[SHIFT + 1 : SHIFT + 2]
    after[...] = value
    unit, _ = normalised(value)
    normed[...] = (unit * vec[GAIN + 1 : GAIN + 2] + vec[SHIFT + 2 : SHIFT + 3]).astype(BF16)


def forward_inner_kernel(normed, pair, vec, partial_out, activated, slope):
    inner = nn(normed[...], pair[0]) + vec[HIDDEN : HIDDEN + 1]
    half = 0.5 + 0.5 * lax.erf(inner * 0.7071067811865476)
    act = (inner * half).astype(BF16)
    activated[...] = act
    slope[...] = half + inner * (jnp.exp(-0.5 * inner * inner) * 0.3989422804014327)
    partial_out[...] = nt(act, pair[1]).astype(partial_out.dtype)


def end_norm_kernel(count, after, vec, next_vec, *refs):
    parts, output = refs[:count], refs[count]
    value = (after[...] + total_of(parts) + vec[SHIFT + 3 : SHIFT + 4]).astype(BF16)
    output[...] = value
    if len(refs) > count + 1:
        unit, _ = normalised(value.astype(F32))
        refs[count + 1][...] = (
            unit * next_vec[GAIN : GAIN + 1] + next_vec[SHIFT : SHIFT + 1]
        ).astype(BF16)


def backward_inner_kernel(delta, pair, slope, partial_out, inner_delta):
    value = (nn(delta[...], pair[1]) * slope[...]).astype(BF16)
    inner_delta[...] = value
    partial_out[...] = nt(value, pair[0]).astype(partial_out.dtype)


def inner_weights_kernel(count, place, *refs):
    normed, inner_delta, delta, activated = (refs[k * count : (k + 1) * count] for k in range(4))
    kept, sent, bias = refs[4 * count :]
    joined = jnp.concatenate([item[...] for item in inner_delta], axis=0)
    bias[...] = jnp.sum(joined.astype(F32), axis=0, keepdims=True)
    core = place[0]
    up = tn(jnp.concatenate([item[...] for item in normed], axis=0), joined).astype(BF16)
    down = tn(
        jnp.concatenate([item[...] for item in delta], axis=0),
        jnp.concatenate([item[...] for item in activated], axis=0),
    ).astype(BF16)
    kept[...] = pick(core, up, down)
    sent[...] = pick(core, down, up)


def norm_pull(delta, values, gain):
    unit, rate = normalised(values)
    scaled = delta * gain
    through = rate * (
        scaled
        - jnp.mean(scaled, axis=-1, keepdims=True)
        - unit * jnp.mean(scaled * unit, axis=-1, keepdims=True)
    )
    return through, jnp.sum(delta * unit, axis=0, keepdims=True), jnp.sum(delta, axis=0, keepdims=True)


def middle_pull_kernel(count, place, delta_out, after, vec, *refs):
    parts, outs, (full, rounded, sums), pieces = (
        refs[:count],
        refs[count : 3 * count],
        refs[3 * count : 3 * count + 3],
        refs[3 * count + 3 :],
    )
    delta = delta_out[...].astype(F32)
    through, gain, shift = norm_pull(total_of(parts), after[...], vec[GAIN + 1 : GAIN + 2])
    value = delta + through
    full[...] = value
    low = value.astype(BF16)
    rounded[...] = low
    half = low.shape[1] // 2
    mine, other = pick(place[0], low[:, :half], low[:, half:]), pick(place[0], low[:, half:], low[:, :half])
    for own, far, piece in zip(outs[:count], outs[count:], pieces):
        piece[...] = (nn(mine, own[...]) + nn(other, far[...])).astype(BF16)
    sums[0:1] = gain
    sums[1:2] = shift
    sums[2:3] = jnp.sum(value, axis=0, keepdims=True)
    sums[3:4] = jnp.sum(delta, axis=0, keepdims=True)
    sums[4:] = jnp.zeros_like(sums[4:])


def first_pull_kernel(count, after_delta, hidden, vec, *refs):
    parts, (full, sums) = refs[:count], refs[count:]
    through, gain, shift = norm_pull(total_of(parts), hidden[...].astype(F32), vec[GAIN : GAIN + 1])
    full[...] = (after_delta[...] + through).astype(full.dtype)
    sums[0:1] = gain
    sums[1:2] = shift
    sums[2:] = jnp.zeros_like(sums[2:])


def attend_pull_kernel(count, keys, values, *refs):
    query, mix_delta, weights, mixed = (refs[k * count : (k + 1) * count] for k in range(4))
    query_delta, keys_delta, values_delta, key_sum, value_sum = refs[4 * count :]
    width = keys.shape[1]
    rows = query[0].shape[0]
    masks = head_masks(width)
    own_keys = [only(mask, keys[...]) for mask in masks]
    for chunk in range(count):
        delta_all = mix_delta[chunk][...]
        product = delta_all.astype(F32) * mixed[chunk][...]
        query_turned, delta_turned = query[chunk][...].T, delta_all.T
        total = None
        for head, mask in enumerate(masks):
            lanes = slice(head * HEAD_DIM, (head + 1) * HEAD_DIM)
            rounded = weights[chunk][head]
            row = jnp.sum(only(mask, product), axis=1, keepdims=True)
            pulled = nt(only(mask, delta_all), values[...])
            scored = (rounded.astype(F32) * (pulled - row)).astype(BF16)
            to_query = nn(scored, own_keys[head])
            total = to_query if total is None else total + to_query
            to_keys = nn(query_turned[lanes], scored)
            to_values = nn(delta_turned[lanes], rounded)
            if chunk == 0:
                key_sum[lanes, :] = to_keys
                value_sum[lanes, :] = to_values
            else:
                key_sum[lanes, :] += to_keys
                value_sum[lanes, :] += to_values
        query_delta[chunk] = (total * SCALE).astype(BF16)
    all_keys, all_values = (key_sum[...] * SCALE).T, value_sum[...].T
    for chunk in range(count):
        part = slice(chunk * rows, (chunk + 1) * rows)
        keys_delta[chunk] = all_keys[part].astype(BF16)
        values_delta[chunk] = all_values[part].astype(BF16)


def project_pull_kernel(chunk, query_delta, keys_delta, values_delta, mix, partial_out):
    total = nt(query_delta[chunk], mix[0])
    total += nt(keys_delta[chunk], mix[1])
    total += nt(values_delta[chunk], mix[2])
    partial_out[...] = total.astype(partial_out.dtype)


def mix_weights_kernel(count, place, query_delta, keys_delta, values_delta, *refs):
    normed, delta, mixed = (refs[k * count : (k + 1) * count] for k in range(3))
    kept, sent, bias = refs[3 * count :]

    def joined(item):
        return jnp.concatenate([item[k] for k in range(count)], axis=0)

    core = place[0]
    rows = jnp.concatenate([item[...] for item in normed], axis=0)
    by_query, by_keys, by_values = joined(query_delta), joined(keys_delta), joined(values_delta)
    of_query, of_keys = tn(rows, by_query).astype(BF16), tn(rows, by_keys).astype(BF16)
    of_values = tn(rows, by_values).astype(BF16)
    of_out = tn(
        jnp.concatenate([item[...] for item in delta], axis=0),
        jnp.concatenate([item[...].astype(BF16) for item in mixed], axis=0),
    ).astype(BF16)
    cols = of_out.shape[1]
    for item, (low, high) in enumerate([(of_query, of_values), (of_keys, of_out)]):
        lanes = slice(item * cols, (item + 1) * cols)
        kept[:, lanes] = pick(core, low, high)
        sent[:, lanes] = pick(core, high, low)
    bias[0:1] = jnp.sum(by_query.astype(F32), axis=0, keepdims=True)
    bias[1:2] = jnp.sum(by_values.astype(F32), axis=0, keepdims=True)


def sums_kernel(place, *refs):
    layers, (kept, sent) = (refs[:4], refs[4:8]), refs[8:]
    core = place[0]
    kept[...] = jnp.zeros_like(kept)
    sent[...] = jnp.zeros_like(sent)

    def put(row, lanes, values):
        kept[row : row + 1, :lanes] = pick(core, values[0], values[1])
        sent[row : row + 1, :lanes] = pick(core, values[1], values[0])

    width = kept.shape[1]
    for row, source, at in ((0, 0, 0), (1, 1, 0), (2, 0, 1), (3, 1, 2), (4, 1, 1), (5, 1, 3)):
        put(row, width, [layer[source][at : at + 1] for layer in layers])
    put(6, layers[0][2].shape[1], [layer[2][...] for layer in layers])
    for kind in range(2):
        put(7 + kind, layers[0][3].shape[1], [layer[3][kind : kind + 1] for layer in layers])


def pieces_kernel(ways, wide, fine, place, kept, received, pieces):
    part = place[2]
    sums = kept[...] + received[...]
    peers = pieces.shape[0] // ways
    pieces[...] = jnp.zeros_like(pieces)
    for owner in range(ways * peers):
        group = owner // peers
        here = part == owner % peers
        pieces[owner, :6, :wide] = sums[:6, owner * wide : (owner + 1) * wide]
        for item in range(sums.shape[1] // 128):
            start = item * 128 + group * (128 // ways)
            pieces[owner, 8 + item : 9 + item, : 128 // ways] = jnp.where(
                here, sums[6:7, start : start + 128 // ways], 0.0
            )
        for item in range(fine):
            start = item * HEAD_DIM + group * (HEAD_DIM // ways)
            for kind in range(2):
                row = kind * fine + item
                pieces[owner, row : row + 1, 64 : 64 + HEAD_DIM // ways] = jnp.where(
                    here, sums[7 + kind : 8 + kind, start : start + HEAD_DIM // ways], 0.0
                )


def stack_kernel(one, two, out):
    rows = one.shape[0]
    out[:rows, :] = one[...]
    out[rows:, :] = two[...]


def assemble_kernel(part, place, held, got, out):
    for step, source in enumerate((held, held, got, got)):
        owner = place[1] ^ (0, 2, 1, 3)[step]
        source_rows = slice((step % 2) * part, (step % 2 + 1) * part)
        out[pl.ds(pl.multiple_of(owner * part, part), part), :] = source[source_rows, :]


def unpack_kernel(place, own, other, *outs):
    core = place[0]
    cols = outs[0].shape[2]
    each = own.shape[1] // cols
    found = [None] * (2 * each)
    for item in range(each):
        lanes = slice(item * cols, (item + 1) * cols)
        found[item] = pick(core, own[:, lanes], other[:, lanes])
        found[each + item] = pick(core, other[:, lanes], own[:, lanes])
    for item in range(outs[0].shape[0]):
        outs[0][item] = found[item]
    if len(outs) > 1:
        half = outs[1].shape[0]
        low, high = found[-1][:half], found[-1][half:]
        outs[1][...] = pick(core, low, high)
        outs[2][...] = pick(core, high, low)


def presum_kernel(kept, received, out):
    out[...] = (kept[...].astype(F32) + received[...].astype(F32)).astype(out.dtype)


def presum_shards_kernel(part, place, kept, received, held, given):
    for step, out in enumerate((held, held, given, given)):
        owner = place[1] ^ (0, 2, 1, 3)[step]
        rows = pl.ds(pl.multiple_of(owner * part, part), part)
        out[(step % 2) * part : (step % 2 + 1) * part, :] = (
            kept[rows, :].astype(F32) + received[rows, :].astype(F32)
        ).astype(out.dtype)


def halfway_kernel(held, got, kept, given):
    part = kept.shape[0]
    kept[...] = held[:part, :] + got[:part, :].astype(F32)
    given[...] = (held[part:, :] + got[part:, :].astype(F32)).astype(BF16)


def final_sum_kernel(*refs):
    refs[-1][...] = total_of(refs[:-1])


def inner_out_kernel(place, kept, got, up, down):
    core = place[0]
    up[0] = pick(core, kept[...], got[...]).astype(F32)
    down[0] = pick(core, got[...], kept[...]).astype(F32)


def mix_out_kernel(place, kept, got, mix, out):
    core = place[0]
    cols = mix.shape[3]
    low = pick(core, kept[...], got[...]).astype(F32)
    high = pick(core, got[...], kept[...]).astype(F32)
    mix[0, 0] = low[:, :cols]
    mix[0, 1] = low[:, cols:]
    mix[0, 2] = high[:, :cols]
    out[0] = high[:, cols:].T


def shares_kernel(pieces, gain, shift, hidden, head):
    total = pieces[0]
    for owner in range(1, pieces.shape[0]):
        total += pieces[owner]
    gain[0] = total[:2, : gain.shape[2]]
    shift[0] = total[2:6, : shift.shape[2]]
    hidden[0] = total[8 : 8 + hidden.shape[1], : hidden.shape[2]]
    fine, each = head.shape[2:]
    for kind in range(2):
        head[0, kind] = total[kind * fine : (kind + 1) * fine, 64 : 64 + each]


def after(value, *others):
    if not others:
        return value
    return lax.optimization_barrier((value,) + others)[0]


def other_core(value):
    return lax.ppermute(value, "section", [(0, 1), (1, 0)])


def to_peer(value, mask, count):
    return lax.ppermute(value, "tensor", [(k, k ^ mask) for k in range(count)])


def along(value, mask):
    return lax.ppermute(value, "dp", [(k, k ^ mask) for k in range(4)])


def on_device(
    tokens,
    cotangent,
    lengths,
    assignment,
    mix_weight,
    head_bias,
    out_weight,
    norm_gain,
    row_shift,
    up_weight,
    hidden_bias,
    down_weight,
):
    peers = lax.axis_size("tensor")
    ways = lax.axis_size("dp")
    micro, rows, width = tokens.shape
    buffer = rows * peers
    heads_width = out_weight.shape[1]
    heads = heads_width // HEAD_DIM
    units = up_weight.shape[2]
    shard = width // ways
    stepped = ways == 4
    order, take, give = (SWITCHES[name] for name in ('order', 'take', 'give'))
    place = jnp.stack([lax.axis_index(axis) for axis in ("section", "dp", "tensor")]).astype(jnp.int32)
    given = (
        place,
        tokens,
        cotangent,
        lengths,
        assignment,
        mix_weight,
        out_weight,
        up_weight,
        jnp.swapaxes(down_weight, 1, 2),
        norm_gain,
        row_shift,
        hidden_bias,
        jnp.swapaxes(head_bias, 1, 2),
    )
    place, tokens, cotangent, lengths, assignment, mix_weight, out_weight = (
        given := lax.optimization_barrier(given)
    )[:7]
    up_weight, turned_down, norm_gain, row_shift, hidden_bias, flat_head = given[7:]

    latest, held, made, pending, count = [], [], {}, {}, [0]

    def run(kernel, outs, *args, smem=0, **options):
        args = list(args)
        if latest or held:
            args[smem] = after(args[smem], *latest, *held)
        done = kernel_call(kernel, outs, *args, smem=smem, **options)
        latest[:] = [jax.tree.leaves(done)[0]]
        held.clear()
        return done

    def main(kernel, *args, **options):
        done = run(kernel, *args, **options)
        count[0] += 1
        return done

    def main_placed(kernel, outs, *args, **options):
        return main(kernel, outs, place, *args, smem=1, **options)

    def step(name):
        def keep(function):
            pending[name] = function
            return function

        return keep

    def need(name):
        if name not in made:
            function = pending.pop(name)
            made[name] = function()
        return made[name]

    def place_of(name):
        return PLACES.get(name, 99)

    def flush():
        for name in sorted(pending, key=place_of):
            if name in pending and place_of(name) <= count[0]:
                need(name)

    def now(value):
        return after(value, *latest)

    def placed(kernel, outs, *args, **options):
        return run(kernel, outs, place, *args, smem=1, **options)

    def scratch_of(*items):
        return [pltpu.VMEM(item.shape, item.dtype) for item in items] + [
            pltpu.SemaphoreType.DMA((len(items),))
        ]

    def picked(one, two, *types):
        return placed(pick_kernel, [shape(one.shape, item) for item in types], one, two, mib=8)

    def collect(chunk):
        got = {step: to_peer(chunk, step, peers) for step in order}
        return [chunk] + [got[step] for step in range(1, peers)]

    def columns(mine, other):
        got = collect(after(mine, *latest))
        return got + [other] + [other_core(item) for item in got[1:]]

    def spread(parts):
        got = {step: to_peer(parts[step], step, peers) for step in order}
        return [parts[0]] + [got[step] for step in range(1, peers)]

    def part_type(step):
        return F32 if step == 0 else BF16

    def gather(half, *before):
        half = after(half, *before)
        return half, along(half, 2) if stepped else lax.all_gather(half, "dp", axis=0, tiled=True)

    def stacked(half, far):
        if not stepped:
            return far, far
        both = run(
            stack_kernel, shape((2 * shard, half.shape[1]), BF16), half, far, mib=4
        )
        return both, along(both, 1)

    def assembled(both, near):
        if not stepped:
            return both
        return placed(
            partial(assemble_kernel, shard), shape((width, both.shape[1]), BF16), both, near, mib=4
        )

    def unpacked(own, items):
        other = other_core(own)
        cols = own.shape[1] // items
        if items == 1:
            outs = shape((2, width, cols), BF16)
        else:
            outs = [shape((3, width, cols), BF16)] + [shape((width // 2, cols), BF16)] * 2
        return placed(unpack_kernel, outs, own, other, mib=8)

    def project(chunk, mix, vec):
        return main(
            project_kernel,
            [shape((rows, heads_width), BF16)] * 3,
            chunk,
            mix,
            vec,
            mib=4,
        )

    def join(projected):
        return main(
            partial(join_kernel, peers),
            [shape((buffer, heads_width), BF16)] * 2,
            *[item[1] for item in projected],
            *[item[2] for item in projected],
            mib=4,
        )

    def attend(step, query, keys, values):
        return main(
            attend_kernel,
            [
                shape((rows, heads_width), F32),
                shape((rows, heads_width), BF16),
                shape((heads, rows, buffer), BF16),
            ],
            query,
            keys,
            values,
            seg_cols[step],
            seg_row,
            mib=8,
        )

    def projections(whole, vec, mix):
        projected = {}
        for item in [0] + take:
            projected[item] = project(whole[item], mix, vec)
            flush()
        return [projected[item] for item in range(peers)]

    def attention(projected):
        keys, values = join(projected)
        flush()
        attended = [None] * peers
        for item in give + [0]:
            attended[item] = attend(item, projected[item][0], keys, values)
            flush()
        query, mixed = [item[0] for item in projected], [item[0] for item in attended]
        kept = (query, keys, values, [item[2] for item in attended], mixed)
        return spread([item[1] for item in attended]), kept

    def middle_norm(hidden, vec, parts, outs):
        return main_placed(
            partial(middle_norm_kernel, peers),
            [shape((rows, width), F32), shape((rows, width), BF16)],
            hidden,
            vec,
            *parts,
            *outs,
            mib=4,
        )

    def forward_inner(step, normed, pair, vec):
        return main(
            forward_inner_kernel,
            [
                shape((rows, width), part_type(step)),
                shape((rows, units), BF16),
                shape((rows, units), F32),
            ],
            normed,
            pair,
            vec,
            mib=8,
        )

    def end_norm(after_rows, vec, next_vec, parts, beside=False):
        return (run if beside else main)(
            partial(end_norm_kernel, peers),
            [shape((rows, width), BF16)] * (1 if next_vec is None else 2),
            after_rows,
            vec,
            vec if next_vec is None else next_vec,
            *parts,
            mib=4,
        )

    def backward_inner(step, delta, pair, slope):
        return main(
            backward_inner_kernel,
            [shape((rows, width), part_type(step)), shape((rows, units), BF16)],
            delta,
            pair,
            slope,
            mib=8,
        )

    def inner_weights(normed, inner_delta, delta, activated):
        return placed(
            partial(inner_weights_kernel, peers),
            [shape((width, units), BF16)] * 2 + [shape((1, units), F32)],
            *normed,
            *inner_delta,
            *delta,
            *activated,
            mib=16,
        )

    def middle_pull(delta, after_rows, vec, parts, outs):
        full, rounded, sums, *pieces = main_placed(
            partial(middle_pull_kernel, peers),
            [shape((rows, width), F32), shape((rows, width), BF16), shape((8, width), F32)]
            + [shape((rows, heads_width), BF16)] * peers,
            delta,
            after_rows,
            vec,
            *parts,
            *outs,
            mib=8,
        )
        return full, rounded, sums, spread(pieces)

    def attention_pull(mix_delta, kept, mix):
        query, keys, values, weights, mixed = kept
        three = main(
            partial(attend_pull_kernel, peers),
            [shape((peers, rows, heads_width), BF16)] * 3,
            keys,
            values,
            *query,
            *mix_delta,
            *weights,
            *mixed,
            scratch=[pltpu.VMEM((heads_width, buffer), F32)] * 2,
            mib=16,
        )
        flush()
        parts = {}
        for item in give + [0]:
            parts[item] = main(
                partial(project_pull_kernel, item),
                shape((rows, width), part_type(item)),
                *three,
                mix,
                mib=4,
            )
            flush()
        return three, spread([parts[item] for item in range(peers)])

    def mix_weights(three, whole, whole_after, mixed):
        return placed(
            partial(mix_weights_kernel, peers),
            [shape((width, 2 * heads_width), BF16)] * 2 + [shape((2, heads_width), F32)],
            *three,
            *whole,
            *whole_after,
            *mixed,
            mib=16,
        )

    def first_pull(after_delta, hidden, vec, parts, dtype):
        return main(
            partial(first_pull_kernel, peers),
            [shape((rows, width), dtype), shape((8, width), F32)],
            after_delta,
            hidden,
            vec,
            *parts,
            mib=8,
        )

    def presummed(kept, got):
        cols = got.shape[1]
        if not stepped:
            both = run(presum_kernel, shape(got.shape, BF16), kept, got, mib=4)
            return [lax.psum_scatter(both, "dp", scatter_dimension=0, tiled=True)]
        held, given = placed(
            partial(presum_shards_kernel, shard),
            [shape((2 * shard, cols), F32), shape((2 * shard, cols), BF16)],
            kept,
            got,
            mib=4,
        )
        return held, along(given, 1)

    def halfway(held, *got):
        if not stepped:
            return [held]
        kept, given = run(
            halfway_kernel,
            [shape((shard, held.shape[1]), F32), shape((shard, held.shape[1]), BF16)],
            held,
            *got,
            mib=4,
        )
        return kept, along(given, 2)

    def settled(parts):
        if not stepped:
            return parts[0].astype(F32)
        return run(final_sum_kernel, shape(parts[0].shape, F32), *parts, mib=4)

    sources = (mix_weight, out_weight)
    mix_own, mix_sent = placed(
        pack_kernel,
        [shape((shard, 2 * heads_width), BF16)] * 2,
        *sources,
        scratch=scratch_of(*sources),
        far=2,
        mib=8,
    )
    mix_got = other_core(mix_sent)
    sources = (tokens, cotangent, norm_gain, row_shift, hidden_bias, up_weight, turned_down)
    entered = run(
        enter_kernel,
        [shape((rows, width), BF16)] * 2
        + [shape((1, buffer), jnp.int32), shape((PACKED, width), F32)]
        + [shape((shard, units), BF16)] * 2
        + [shape((rows, 1), jnp.int32)] * peers,
        place,
        lengths,
        assignment,
        flat_head,
        *sources,
        scratch=scratch_of(*sources),
        smem=3,
        far=7,
        mib=8,
    )
    entering, pushed, seg_row, vec_own, inner_own, inner_sent = entered[:6]
    seg_cols = entered[6:]
    vec_got, inner_got = other_core(vec_own), other_core(inner_sent)
    mix_halves = picked(mix_own, mix_got, BF16, BF16)
    halfway_mix = gather(mix_halves[0])
    vecs = picked(vec_own, vec_got, F32, F32)
    normed = run(first_norm_kernel, shape((rows, width), BF16), entering, vecs[0], mib=4)
    whole_one = collect(normed)
    halfway_mix = stacked(*halfway_mix)
    inner_halves = picked(after(inner_own, *whole_one[1 : 1 + SWITCHES["first"]]), inner_got, BF16, BF16)
    mix_one = assembled(*halfway_mix)

    def weights(name, half, before, items):
        @step(name + "_far")
        def far():
            if before:
                need(before)
            return gather(now(half))

        @step(name + "_stack")
        def stack():
            return stacked(*need(name + "_far"))

        @step(name + "_join")
        def joined():
            return assembled(*need(name + "_stack"))

        @step(name)
        def unpack():
            return unpacked(need(name + "_join"), items)

    weights("inner1", inner_halves[0], None, 1)
    weights("mix2", mix_halves[1], "inner1_far", 2)
    weights("inner2", inner_halves[1], "mix2_far", 1)

    @step("push")
    def push():
        return collect(now(after(pushed, *whole_one[1:])))

    def hold(name, first=1):
        @step(name + "_held")
        def keep():
            held.extend(need(name)[first:])

    def gradient(name, parts):
        step(name + "_parts")(parts)

        @step(name + "_given")
        def exchange():
            return other_core(now(need(name + "_parts")[1]))

        @step(name + "_sum")
        def presum():
            given = need(name + "_given")
            return presummed(need(name + "_parts")[0], given)

        @step(name + "_half")
        def half():
            return halfway(*need(name + "_sum"))

        @step(name)
        def total():
            return settled(need(name + "_half"))

        hold(name + "_sum")
        hold(name + "_half")

    hold("push")
    hold("inner1_far")
    hold("mix2_far")
    hold("inner2_far")
    flush()
    mix_one, *out_one = unpacked(mix_one, 2)

    @step("out1")
    def outs_one():
        return columns(*out_one)

    hold("out1")
    flush()
    projected = projections(whole_one, vecs[0], mix_one)
    parts, kept_one = attention(projected)
    after_one, normed = middle_norm(entering, vecs[0], parts, need("out1"))
    whole_inner_one = collect(normed)
    flush()
    pair_one = need("inner1")
    inner_one = {}
    for item in [0] + take:
        inner_one[item] = forward_inner(item, whole_inner_one[item], pair_one, vecs[0])
        flush()
    parts = spread([inner_one[item][0] for item in range(peers)])
    output_one, normed = end_norm(after_one, vecs[0], vecs[1], parts)
    whole_two = collect(normed)
    flush()

    mix_two, *out_two = need("mix2")

    @step("out2")
    def outs_two():
        return columns(*out_two)

    hold("out2")
    flush()
    projected = projections(whole_two, vecs[1], mix_two)
    parts, kept_two = attention(projected)
    after_two, normed = middle_norm(output_one, vecs[1], parts, need("out2"))
    whole_inner_two = collect(normed)
    flush()
    pair_two = need("inner2")
    whole_push = need("push")
    inner_two, pulled = {}, {}
    for item in [0] + take:
        inner_two[item] = forward_inner(item, whole_inner_two[item], pair_two, vecs[1])
        pulled[item] = backward_inner(item, whole_push[item], pair_two, inner_two[item][2])
        flush()
    parts = spread([pulled[item][0] for item in range(peers)])
    pulled_two = pulled

    def inner_weights_two():
        return inner_weights(
            whole_inner_two,
            [pulled_two[item][1] for item in range(peers)],
            whole_push,
            [inner_two[item][1] for item in range(peers)],
        )

    gradient("d_inner2", inner_weights_two)
    flush()
    after_delta, rounded_two, sums_middle, mix_delta = middle_pull(
        pushed, after_two, vecs[1], parts, need("out2")
    )

    @step("after2")
    def whole_after_two():
        return collect(now(rounded_two))


    @step("late")
    def late():
        return spread([now(inner_two[item][0]) for item in range(peers)])

    hold("late")
    @step("late_end")
    def late_end():
        parts = need("late")
        (output_two,) = end_norm(after_two, vecs[1], None, parts, beside=True)
        return picked(output_one, output_two, BF16, BF16)

    @step("late_given")
    def late_given():
        return other_core(now(need("late_end")[1]))

    flush()
    three, parts = attention_pull(mix_delta, kept_two, mix_two)
    three_two = three
    gradient("d_mix2", lambda: mix_weights(three_two, whole_two, need("after2"), kept_two[4]))
    flush()
    delta_two, sums_first = first_pull(after_delta, output_one, vecs[1], parts, BF16)
    sums_two = (sums_first, sums_middle)
    whole_delta = collect(delta_two)
    flush()

    pulled = {}
    for item in [0] + take:
        pulled[item] = backward_inner(item, whole_delta[item], pair_one, inner_one[item][2])
        flush()
    parts = spread([pulled[item][0] for item in range(peers)])
    pulled_one = pulled

    def inner_weights_one():
        return inner_weights(
            whole_inner_one,
            [pulled_one[item][1] for item in range(peers)],
            whole_delta,
            [inner_one[item][1] for item in range(peers)],
        )

    gradient("d_inner1", inner_weights_one)
    flush()
    after_delta, rounded_one, sums_middle, mix_delta = middle_pull(
        delta_two, after_one, vecs[0], parts, need("out1")
    )

    @step("after1")
    def whole_after_one():
        return collect(now(rounded_one))

    flush()
    three, parts = attention_pull(mix_delta, kept_one, mix_one)
    three_one = three
    gradient("d_mix1", lambda: mix_weights(three_one, whole_one, need("after1"), kept_one[4]))
    flush()
    delta_one, sums_first = first_pull(after_delta, entering, vecs[0], parts, F32)
    sums_one = (sums_first, sums_middle)

    def by_core(kept, got):
        return placed(place_kernel, shape((1, 2) + kept.shape, kept.dtype), kept, got, mib=8)

    @step("sums")
    def sums():
        vectors = []
        for number, layer in (("1", sums_one), ("2", sums_two)):
            vectors += [*layer, need("d_inner" + number + "_parts")[2], need("d_mix" + number + "_parts")[2]]
        kept, given = placed(sums_kernel, [shape((PACKED, width), F32)] * 2, *vectors, mib=4)
        return kept, other_core(given)

    @step("pieces")
    def pieces():
        return placed(
            partial(pieces_kernel, ways, width // (ways * peers), heads),
            shape((ways * peers, 16, 128), F32),
            *need("sums"),
            mib=4,
        )

    @step("shares")
    def shares():
        return run(
            shares_kernel,
            [
                shape((1, 2, width // (ways * peers)), F32),
                shape((1, 4, width // (ways * peers)), F32),
                shape((1, units // 128, 128 // ways), F32),
                shape((1, 2, heads, HEAD_DIM // ways), F32),
            ],
            lax.all_to_all(need("pieces"), ("dp", "tensor"), 0, 0, tiled=True),
            mib=4,
        )

    @step("delta")
    def delta():
        kept, given = picked(delta_one, delta_two, F32, F32)
        return kept, other_core(given)

    @step("delta_out")
    def delta_out():
        return by_core(*need("delta"))

    @step("late_out")
    def late_out():
        return by_core(need("late_end")[0], need("late_given"))

    @step("inner_given")
    def inner_total():
        kept, given = picked(need("d_inner1"), need("d_inner2"), F32, F32)
        return kept, other_core(given)

    @step("inner_out")
    def inner_out():
        return placed(
            inner_out_kernel, [shape((1, shard, units), F32)] * 2, *need("inner_given"), mib=4
        )

    @step("mix_given")
    def mix_total():
        kept, given = picked(need("d_mix1"), need("d_mix2"), F32, F32)
        return kept, other_core(given)

    @step("mix_out")
    def mix_out():
        return placed(
            mix_out_kernel,
            [shape((1, 3, shard, heads_width), F32), shape((1, heads_width, shard), F32)],
            *need("mix_given"),
            mib=4,
        )

    for name in sorted(pending, key=place_of):
        if not name.endswith("_held"):
            need(name)
    gain_gradient, shift_gradient, hidden_gradient, head_gradient = made["shares"]
    layer_output, input_gradient = made["late_out"], made["delta_out"]
    mix_gradient, out_gradient = made["mix_out"]
    up_gradient, down_gradient = made["inner_out"]
    return (
        layer_output,
        input_gradient,
        mix_gradient,
        head_gradient,
        out_gradient,
        gain_gradient,
        shift_gradient,
        up_gradient,
        hidden_gradient,
        jnp.swapaxes(down_gradient, 1, 2),
    )


def solution(mesh):
    placed = (
        P(None, ("dp", "tensor"), None),
        P(None, ("dp", "tensor"), None),
        P("dp", None),
        P("dp", None),
        P("section", None, "dp", "tensor"),
        P("section", None, "tensor", None),
        P("section", "tensor", "dp"),
        P("section", None, None),
        P("section", None, None),
        P("section", "dp", "tensor"),
        P("section", "tensor", None),
        P("section", "tensor", "dp"),
    )
    return jax.shard_map(
        on_device,
        mesh=mesh,
        in_specs=placed,
        out_specs=(
            P("section", None, ("dp", "tensor"), None),
            P("section", None, ("dp", "tensor"), None),
            P("section", None, "dp", "tensor"),
            P("section", None, "tensor", "dp"),
            P("section", "tensor", "dp"),
            P("section", None, ("dp", "tensor")),
            P("section", None, ("dp", "tensor")),
            P("section", "dp", "tensor"),
            P("section", "tensor", "dp"),
            P("section", "tensor", "dp"),
        ),
        check_vma=False,
    )
```

```python
from functools import partial

import jax
import jax.numpy as jnp
from jax import lax
from jax.experimental import pallas as pl
from jax.experimental.pallas import tpu as pltpu
from jax.sharding import PartitionSpec as P

HEAD_DIM = 64
EPS = 1e-05
F32 = jnp.float32
BF16 = jnp.bfloat16
SCALE = HEAD_DIM ** (-0.5)
PER_US = 1.1e9
COSTS = dict(
    other=0.5,
    project=0.084,
    attend=1.5,
    forward_inner=0.56,
    backward_inner=0.8,
    inner_weights=15,
    mix_delta=0.9,
    attend_pull=2.3,
    project_pull=0.608,
    mix_weights=2.1,
    stack=0.45,
    middle_norm=1.05,
    end_norm=1.5,
    middle_pull=0.75,
    first_pull=1.5,
    presum_shards=0.75,
    halfway=0.15,
    final_sum=0.525,
    join=1.5,
    unpack=0.8,
    assemble=0.5,
    first_norm=0.022,
    enter=6.0,
)
SWITCHES = dict(
    first=3,
    order=[1, 3, 2],
    take=[2, 1, 3],
    give=[2, 1, 3],
    early=0,
    calm=1,
)
PLACES = dict(
    inner1_far=0.0,
    inner1_stack=5.0,
    inner1_join=10.0,
    inner1=13.5,
    push=0,
    mix2_far=10.0,
    mix2_stack=13.0,
    mix2_join=16.0,
    mix2=32.5,
    inner2_far=9.2,
    inner2_stack=18.0,
    inner2_join=25.0,
    inner2=25.5,
    d_inner2_given=34.0,
    d_inner2_sum=34.8,
    d_inner2_half=41.0,
    d_inner2=50.0,
    late=45.8,
    late_end=52.0,
    late_given=50.842,
    d_mix2_given=40.0,
    d_mix2_sum=39.0,
    d_mix2_half=43.0,
    d_mix2=52.148,
    d_inner1_given=45.0,
    d_inner1_sum=44.8,
    d_inner1_half=50.68,
    d_inner1=51.814,
    d_mix1_given=48.8,
    d_mix1_sum=51.063,
    d_mix1_half=51.589,
    d_mix1=51.722,
    sums=52.189,
    delta=47.945,
    pieces=51.45,
    shares=51.85,
    delta_out=51.6,
    late_out=51.65,
    inner_given=51.41,
    inner_out=51.697,
    mix_given=52.266,
    mix_out=52.5,
    out1=0.2,
    out2=16.6,
    after2=34.0,
    after1=42.0,
    out1_held=6,
    out2_held=22.0,
    d_mix2_half_held=44.6,
    d_mix1_half_held=50.937,
    d_mix2_sum_held=47.0,
    push_held=9.0,
    mix2_far_held=17.0,
    inner1_far_held=5.0,
    d_inner2_parts=33,
    d_mix2_parts=36,
    d_inner1_parts=45,
    d_mix1_parts=48,
    d_inner1_sum_held=52.0,
    d_mix1_sum_held=52.0,
)
GAIN, SHIFT, HIDDEN, QUERY_BIAS, VALUE_BIAS, PACKED = 0, 2, 6, 7, 8, 16


def name_of(kernel):
    return getattr(kernel, "func", kernel).__name__[: -len("_kernel")]


def shape(dims, dtype):
    return jax.ShapeDtypeStruct(tuple(dims), dtype)


def kernel_call(kernel, outs, *args, scratch=(), smem=0, far=0, mib=16):
    near = len(args) - far
    args = args[:near] + tuple(pltpu.with_memory_space_constraint(item, pltpu.HBM) for item in args[near:])
    specs = [pl.BlockSpec(memory_space=pltpu.SMEM)] * smem
    specs += [pl.BlockSpec(memory_space=pltpu.VMEM)] * (len(args) - smem - far)
    specs += [pl.BlockSpec(memory_space=pltpu.HBM)] * far
    return pl.pallas_call(
        kernel,
        name='K_'+name_of(kernel),
        out_shape=outs,
        in_specs=specs,
        out_specs=jax.tree.map(lambda _: pl.BlockSpec(memory_space=pltpu.VMEM), outs),
        scratch_shapes=scratch,
        compiler_params=pltpu.CompilerParams(vmem_limit_bytes=mib << 20),
        cost_estimate=pl.CostEstimate(flops=int(COSTS.get(name_of(kernel), COSTS['other']) * PER_US), bytes_accessed=1, transcendentals=0),
    )(*args)


def dot(left, right, left_dim, right_dim):
    return lax.dot_general(
        left, right, (((left_dim,), (right_dim,)), ((), ())), preferred_element_type=F32
    )


def nn(left, right):
    return dot(left, right, 1, 0)


def nt(left, right):
    return dot(left, right, 1, 1)


def tn(left, right):
    return dot(left, right, 0, 0)


def normalised(values):
    centre = values - jnp.mean(values, axis=-1, keepdims=True)
    rate = lax.rsqrt(jnp.mean(centre * centre, axis=-1, keepdims=True) + EPS)
    return centre * rate, rate


def head_masks(width):
    lane = lax.broadcasted_iota(jnp.int32, (1, width), 1) // HEAD_DIM
    return [lane == head for head in range(width // HEAD_DIM)]


def only(mask, values):
    return jnp.where(mask, values, jnp.zeros_like(values))


def total_of(parts):
    total = parts[0][...].astype(F32)
    for part in parts[1:]:
        total = total + part[...].astype(F32)
    return total


def pick(core, one, two):
    return jnp.where(core == 0, one, two)


def fetch(sources, held, sems):
    copies = [
        pltpu.make_async_copy(source, target, sems.at[k])
        for k, (source, target) in enumerate(zip(sources, held))
    ]
    for copy in copies:
        copy.start()
    return copies


def enter_kernel(place, lengths, belongs, head, *refs):
    sources, refs = refs[:7], refs[7:]
    entering, pushed, seg_row, vec, inner_own, inner_sent = refs[:6]
    seg_cols, held, sems = refs[6:-8], refs[-8:-1], refs[-1]
    copies = fetch(sources, held, sems)
    tokens, cotangent, gain, shift, hidden, up, down = held
    core, part = place[0], place[2]
    rows, slots, buffer = tokens.shape[1], lengths.shape[1], seg_row.shape[1]
    lane = lax.broadcasted_iota(jnp.int32, (1, buffer), 1)
    row_place = lane
    col_places = []
    for step in range(buffer // rows):
        shifted = ((part ^ step) - step) * rows
        row_place = jnp.where(
            (lane >= step * rows) & (lane < (step + 1) * rows), lane + shifted, row_place
        )
        col_places.append(lax.broadcasted_iota(jnp.int32, (rows, 1), 0) + (part ^ step) * rows)
    places = [row_place] + col_places
    found = [jnp.full(item.shape, slots, jnp.int32) for item in places]
    for slot in range(slots):
        start = jnp.int32(0)
        for other in range(slot):
            start += jnp.where(belongs[0, other] == belongs[0, slot], lengths[0, other], 0)
        stop = jnp.where(belongs[0, slot] == core, start + lengths[0, slot], start)
        found = [
            jnp.where((item >= start) & (item < stop), slot, kept) for item, kept in zip(places, found)
        ]
    seg_row[...] = found[0]
    for out, item in zip(seg_cols, found[1:]):
        out[...] = item
    for copy in copies:
        copy.wait()
    entering[...] = tokens[core]
    push = cotangent[core].astype(F32)
    pushed[...] = jnp.where(found[1] != slots, push, 0.0).astype(BF16)
    vec[...] = jnp.zeros_like(vec)
    vec[GAIN : GAIN + 2] = gain[0].astype(F32)
    vec[SHIFT : SHIFT + 4] = shift[0].astype(F32)
    for item in range(hidden.shape[1]):
        lanes = slice(item * 128, (item + 1) * 128)
        vec[HIDDEN : HIDDEN + 1, lanes] = hidden[0, item : item + 1].astype(F32)
    for item in range(head.shape[1]):
        lanes = slice(item * HEAD_DIM, (item + 1) * HEAD_DIM)
        vec[QUERY_BIAS : QUERY_BIAS + 2, lanes] = head[0, item].astype(F32)
    inner_own[...] = pick(core, up[0], down[0])
    inner_sent[...] = pick(core, down[0], up[0])


def pack_kernel(place, *refs):
    sources, (own, sent), held, sems = refs[:2], refs[2:4], refs[4:6], refs[6]
    for copy in fetch(sources, held, sems):
        copy.wait()
    mix, out_weight = held
    core = place[0]
    turned = out_weight[0].T
    cols = turned.shape[1]
    for item, (low, high) in enumerate([(mix[0, 0], mix[0, 2]), (mix[0, 1], turned)]):
        lanes = slice(item * cols, (item + 1) * cols)
        own[:, lanes] = pick(core, low, high)
        sent[:, lanes] = pick(core, high, low)


def pick_kernel(place, one, two, *outs):
    core = place[0]
    outs[0][...] = pick(core, one[...], two[...]).astype(outs[0].dtype)
    outs[1][...] = pick(core, two[...], one[...]).astype(outs[1].dtype)


def place_kernel(place, kept, got, out):
    core = place[0]
    out[0, core] = kept[...].astype(out.dtype)
    out[0, 1 - core] = got[...].astype(out.dtype)


def first_norm_kernel(hidden, vec, normed):
    unit, _ = normalised(hidden[...].astype(F32))
    normed[...] = (unit * vec[GAIN : GAIN + 1] + vec[SHIFT : SHIFT + 1]).astype(BF16)


def project_kernel(normed, mix, vec, query, keys, values):
    width = query.shape[1]
    rows = normed[...]
    query[...] = (nn(rows, mix[0]) + vec[QUERY_BIAS : QUERY_BIAS + 1, :width]).astype(BF16)
    keys[...] = nn(rows, mix[1]).astype(BF16)
    values[...] = (nn(rows, mix[2]) + vec[VALUE_BIAS : VALUE_BIAS + 1, :width]).astype(BF16)


def join_kernel(count, *refs):
    for kind in range(2):
        refs[2 * count + kind][...] = jnp.concatenate(
            [item[...] for item in refs[kind * count : (kind + 1) * count]], axis=0
        )


def attend_kernel(query, keys, values, seg_col, seg_row, mixed, rounded, weights):
    masks = head_masks(query.shape[1])
    barred = jnp.where(seg_col[...] == seg_row[...], 0.0, -1e30)
    scaled = query[...] * jnp.asarray(SCALE, BF16)
    total = None
    for head, mask in enumerate(masks):
        scores = nt(only(mask, scaled), keys[...]) + barred
        lifted = jnp.exp(scores - jnp.max(scores, axis=1, keepdims=True))
        attention = (lifted * (1.0 / jnp.sum(lifted, axis=1, keepdims=True))).astype(BF16)
        weights[head] = attention
        part = nn(attention, only(mask, values[...]))
        total = part if total is None else total + part
    mixed[...] = total
    rounded[...] = total.astype(BF16)


def middle_norm_kernel(count, place, hidden, vec, *refs):
    mixed, outs, (after, normed) = refs[:count], refs[count : 3 * count], refs[3 * count :]
    mine = sum(nt(part[...], out[...]) for part, out in zip(mixed, outs[:count]))
    other = sum(nt(part[...], out[...]) for part, out in zip(mixed, outs[count:]))
    core = place[0]
    value = jnp.concatenate([pick(core, mine, other), pick(core, other, mine)], axis=1)
    value = value + hidden[...].astype(F32) + vec[SHIFT + 1 : SHIFT + 2]
    after[...] = value
    unit, _ = normalised(value)
    normed[...] = (unit * vec[GAIN + 1 : GAIN + 2] + vec[SHIFT + 2 : SHIFT + 3]).astype(BF16)


def forward_inner_kernel(normed, pair, vec, partial_out, activated, slope):
    inner = nn(normed[...], pair[0]) + vec[HIDDEN : HIDDEN + 1]
    half = 0.5 + 0.5 * lax.erf(inner * 0.7071067811865476)
    act = (inner * half).astype(BF16)
    activated[...] = act
    slope[...] = half + inner * (jnp.exp(-0.5 * inner * inner) * 0.3989422804014327)
    partial_out[...] = nt(act, pair[1]).astype(partial_out.dtype)


def end_norm_kernel(count, after, vec, next_vec, *refs):
    parts, output = refs[:count], refs[count]
    value = (after[...] + total_of(parts) + vec[SHIFT + 3 : SHIFT + 4]).astype(BF16)
    output[...] = value
    if len(refs) > count + 1:
        unit, _ = normalised(value.astype(F32))
        refs[count + 1][...] = (
            unit * next_vec[GAIN : GAIN + 1] + next_vec[SHIFT : SHIFT + 1]
        ).astype(BF16)


def backward_inner_kernel(delta, pair, slope, partial_out, inner_delta):
    value = (nn(delta[...], pair[1]) * slope[...]).astype(BF16)
    inner_delta[...] = value
    partial_out[...] = nt(value, pair[0]).astype(partial_out.dtype)


def inner_weights_kernel(count, place, *refs):
    normed, inner_delta, delta, activated = (refs[k * count : (k + 1) * count] for k in range(4))
    kept, sent, bias = refs[4 * count :]
    joined = jnp.concatenate([item[...] for item in inner_delta], axis=0)
    bias[...] = jnp.sum(joined.astype(F32), axis=0, keepdims=True)
    core = place[0]
    up = tn(jnp.concatenate([item[...] for item in normed], axis=0), joined).astype(BF16)
    down = tn(
        jnp.concatenate([item[...] for item in delta], axis=0),
        jnp.concatenate([item[...] for item in activated], axis=0),
    ).astype(BF16)
    kept[...] = pick(core, up, down)
    sent[...] = pick(core, down, up)


def norm_pull(delta, values, gain):
    unit, rate = normalised(values)
    scaled = delta * gain
    through = rate * (
        scaled
        - jnp.mean(scaled, axis=-1, keepdims=True)
        - unit * jnp.mean(scaled * unit, axis=-1, keepdims=True)
    )
    return through, jnp.sum(delta * unit, axis=0, keepdims=True), jnp.sum(delta, axis=0, keepdims=True)


def middle_pull_kernel(count, place, delta_out, after, vec, *refs):
    parts, outs, (full, rounded, sums), pieces = (
        refs[:count],
        refs[count : 3 * count],
        refs[3 * count : 3 * count + 3],
        refs[3 * count + 3 :],
    )
    delta = delta_out[...].astype(F32)
    through, gain, shift = norm_pull(total_of(parts), after[...], vec[GAIN + 1 : GAIN + 2])
    value = delta + through
    full[...] = value
    low = value.astype(BF16)
    rounded[...] = low
    half = low.shape[1] // 2
    mine, other = pick(place[0], low[:, :half], low[:, half:]), pick(place[0], low[:, half:], low[:, :half])
    for own, far, piece in zip(outs[:count], outs[count:], pieces):
        piece[...] = (nn(mine, own[...]) + nn(other, far[...])).astype(BF16)
    sums[0:1] = gain
    sums[1:2] = shift
    sums[2:3] = jnp.sum(value, axis=0, keepdims=True)
    sums[3:4] = jnp.sum(delta, axis=0, keepdims=True)
    sums[4:] = jnp.zeros_like(sums[4:])


def first_pull_kernel(count, after_delta, hidden, vec, *refs):
    parts, (full, sums) = refs[:count], refs[count:]
    through, gain, shift = norm_pull(total_of(parts), hidden[...].astype(F32), vec[GAIN : GAIN + 1])
    full[...] = (after_delta[...] + through).astype(full.dtype)
    sums[0:1] = gain
    sums[1:2] = shift
    sums[2:] = jnp.zeros_like(sums[2:])


def attend_pull_kernel(count, keys, values, *refs):
    query, mix_delta, weights, mixed = (refs[k * count : (k + 1) * count] for k in range(4))
    query_delta, keys_delta, values_delta, key_sum, value_sum = refs[4 * count :]
    width = keys.shape[1]
    rows = query[0].shape[0]
    masks = head_masks(width)
    own_keys = [only(mask, keys[...]) for mask in masks]
    for chunk in range(count):
        delta_all = mix_delta[chunk][...]
        product = delta_all.astype(F32) * mixed[chunk][...]
        query_turned, delta_turned = query[chunk][...].T, delta_all.T
        total = None
        for head, mask in enumerate(masks):
            lanes = slice(head * HEAD_DIM, (head + 1) * HEAD_DIM)
            rounded = weights[chunk][head]
            row = jnp.sum(only(mask, product), axis=1, keepdims=True)
            pulled = nt(only(mask, delta_all), values[...])
            scored = (rounded.astype(F32) * (pulled - row)).astype(BF16)
            to_query = nn(scored, own_keys[head])
            total = to_query if total is None else total + to_query
            to_keys = nn(query_turned[lanes], scored)
            to_values = nn(delta_turned[lanes], rounded)
            if chunk == 0:
                key_sum[lanes, :] = to_keys
                value_sum[lanes, :] = to_values
            else:
                key_sum[lanes, :] += to_keys
                value_sum[lanes, :] += to_values
        query_delta[chunk] = (total * SCALE).astype(BF16)
    all_keys, all_values = (key_sum[...] * SCALE).T, value_sum[...].T
    for chunk in range(count):
        part = slice(chunk * rows, (chunk + 1) * rows)
        keys_delta[chunk] = all_keys[part].astype(BF16)
        values_delta[chunk] = all_values[part].astype(BF16)


def project_pull_kernel(chunk, query_delta, keys_delta, values_delta, mix, partial_out):
    total = nt(query_delta[chunk], mix[0])
    total += nt(keys_delta[chunk], mix[1])
    total += nt(values_delta[chunk], mix[2])
    partial_out[...] = total.astype(partial_out.dtype)


def mix_weights_kernel(count, place, query_delta, keys_delta, values_delta, *refs):
    normed, delta, mixed = (refs[k * count : (k + 1) * count] for k in range(3))
    kept, sent, bias = refs[3 * count :]

    def joined(item):
        return jnp.concatenate([item[k] for k in range(count)], axis=0)

    core = place[0]
    rows = jnp.concatenate([item[...] for item in normed], axis=0)
    by_query, by_keys, by_values = joined(query_delta), joined(keys_delta), joined(values_delta)
    of_query, of_keys = tn(rows, by_query).astype(BF16), tn(rows, by_keys).astype(BF16)
    of_values = tn(rows, by_values).astype(BF16)
    of_out = tn(
        jnp.concatenate([item[...] for item in delta], axis=0),
        jnp.concatenate([item[...].astype(BF16) for item in mixed], axis=0),
    ).astype(BF16)
    cols = of_out.shape[1]
    for item, (low, high) in enumerate([(of_query, of_values), (of_keys, of_out)]):
        lanes = slice(item * cols, (item + 1) * cols)
        kept[:, lanes] = pick(core, low, high)
        sent[:, lanes] = pick(core, high, low)
    bias[0:1] = jnp.sum(by_query.astype(F32), axis=0, keepdims=True)
    bias[1:2] = jnp.sum(by_values.astype(F32), axis=0, keepdims=True)


def sums_kernel(place, *refs):
    layers, (kept, sent) = (refs[:4], refs[4:8]), refs[8:]
    core = place[0]
    kept[...] = jnp.zeros_like(kept)
    sent[...] = jnp.zeros_like(sent)

    def put(row, lanes, values):
        kept[row : row + 1, :lanes] = pick(core, values[0], values[1])
        sent[row : row + 1, :lanes] = pick(core, values[1], values[0])

    width = kept.shape[1]
    for row, source, at in ((0, 0, 0), (1, 1, 0), (2, 0, 1), (3, 1, 2), (4, 1, 1), (5, 1, 3)):
        put(row, width, [layer[source][at : at + 1] for layer in layers])
    put(6, layers[0][2].shape[1], [layer[2][...] for layer in layers])
    for kind in range(2):
        put(7 + kind, layers[0][3].shape[1], [layer[3][kind : kind + 1] for layer in layers])


def pieces_kernel(ways, wide, fine, place, kept, received, pieces):
    part = place[2]
    sums = kept[...] + received[...]
    peers = pieces.shape[0] // ways
    pieces[...] = jnp.zeros_like(pieces)
    for owner in range(ways * peers):
        group = owner // peers
        here = part == owner % peers
        pieces[owner, :6, :wide] = sums[:6, owner * wide : (owner + 1) * wide]
        for item in range(sums.shape[1] // 128):
            start = item * 128 + group * (128 // ways)
            pieces[owner, 8 + item : 9 + item, : 128 // ways] = jnp.where(
                here, sums[6:7, start : start + 128 // ways], 0.0
            )
        for item in range(fine):
            start = item * HEAD_DIM + group * (HEAD_DIM // ways)
            for kind in range(2):
                row = kind * fine + item
                pieces[owner, row : row + 1, 64 : 64 + HEAD_DIM // ways] = jnp.where(
                    here, sums[7 + kind : 8 + kind, start : start + HEAD_DIM // ways], 0.0
                )


def stack_kernel(one, two, out):
    rows = one.shape[0]
    out[:rows, :] = one[...]
    out[rows:, :] = two[...]


def assemble_kernel(part, place, held, got, out):
    for step, source in enumerate((held, held, got, got)):
        owner = place[1] ^ (0, 2, 1, 3)[step]
        source_rows = slice((step % 2) * part, (step % 2 + 1) * part)
        out[pl.ds(pl.multiple_of(owner * part, part), part), :] = source[source_rows, :]


def unpack_kernel(place, own, other, *outs):
    core = place[0]
    cols = outs[0].shape[2]
    each = own.shape[1] // cols
    found = [None] * (2 * each)
    for item in range(each):
        lanes = slice(item * cols, (item + 1) * cols)
        found[item] = pick(core, own[:, lanes], other[:, lanes])
        found[each + item] = pick(core, other[:, lanes], own[:, lanes])
    for item in range(outs[0].shape[0]):
        outs[0][item] = found[item]
    if len(outs) > 1:
        half = outs[1].shape[0]
        low, high = found[-1][:half], found[-1][half:]
        outs[1][...] = pick(core, low, high)
        outs[2][...] = pick(core, high, low)


def presum_kernel(kept, received, out):
    out[...] = (kept[...].astype(F32) + received[...].astype(F32)).astype(out.dtype)


def presum_shards_kernel(part, place, kept, received, held, given):
    for step, out in enumerate((held, held, given, given)):
        owner = place[1] ^ (0, 2, 1, 3)[step]
        rows = pl.ds(pl.multiple_of(owner * part, part), part)
        out[(step % 2) * part : (step % 2 + 1) * part, :] = (
            kept[rows, :].astype(F32) + received[rows, :].astype(F32)
        ).astype(out.dtype)


def halfway_kernel(held, got, kept, given):
    part = kept.shape[0]
    kept[...] = held[:part, :] + got[:part, :].astype(F32)
    given[...] = (held[part:, :] + got[part:, :].astype(F32)).astype(BF16)


def final_sum_kernel(*refs):
    refs[-1][...] = total_of(refs[:-1])


def inner_out_kernel(place, kept, got, up, down):
    core = place[0]
    up[0] = pick(core, kept[...], got[...]).astype(F32)
    down[0] = pick(core, got[...], kept[...]).astype(F32)


def mix_out_kernel(place, kept, got, mix, out):
    core = place[0]
    cols = mix.shape[3]
    low = pick(core, kept[...], got[...]).astype(F32)
    high = pick(core, got[...], kept[...]).astype(F32)
    mix[0, 0] = low[:, :cols]
    mix[0, 1] = low[:, cols:]
    mix[0, 2] = high[:, :cols]
    out[0] = high[:, cols:].T


def shares_kernel(pieces, gain, shift, hidden, head):
    total = pieces[0]
    for owner in range(1, pieces.shape[0]):
        total += pieces[owner]
    gain[0] = total[:2, : gain.shape[2]]
    shift[0] = total[2:6, : shift.shape[2]]
    hidden[0] = total[8 : 8 + hidden.shape[1], : hidden.shape[2]]
    fine, each = head.shape[2:]
    for kind in range(2):
        head[0, kind] = total[kind * fine : (kind + 1) * fine, 64 : 64 + each]


def after(value, *others):
    if not others:
        return value
    return lax.optimization_barrier((value,) + others)[0]


def other_core(value):
    return lax.ppermute(value, "section", [(0, 1), (1, 0)])


def to_peer(value, mask, count):
    return lax.ppermute(value, "tensor", [(k, k ^ mask) for k in range(count)])


def along(value, mask):
    return lax.ppermute(value, "dp", [(k, k ^ mask) for k in range(4)])


def on_device(
    tokens,
    cotangent,
    lengths,
    assignment,
    mix_weight,
    head_bias,
    out_weight,
    norm_gain,
    row_shift,
    up_weight,
    hidden_bias,
    down_weight,
):
    peers = lax.axis_size("tensor")
    ways = lax.axis_size("dp")
    micro, rows, width = tokens.shape
    buffer = rows * peers
    heads_width = out_weight.shape[1]
    heads = heads_width // HEAD_DIM
    units = up_weight.shape[2]
    shard = width // ways
    stepped = ways == 4
    order, take, give = (SWITCHES[name] for name in ('order', 'take', 'give'))
    place = jnp.stack([lax.axis_index(axis) for axis in ("section", "dp", "tensor")]).astype(jnp.int32)
    given = (
        place,
        tokens,
        cotangent,
        lengths,
        assignment,
        mix_weight,
        out_weight,
        up_weight,
        jnp.swapaxes(down_weight, 1, 2),
        norm_gain,
        row_shift,
        hidden_bias,
        jnp.swapaxes(head_bias, 1, 2),
    )
    place, tokens, cotangent, lengths, assignment, mix_weight, out_weight = (
        given := lax.optimization_barrier(given)
    )[:7]
    up_weight, turned_down, norm_gain, row_shift, hidden_bias, flat_head = given[7:]

    latest, held, made, pending, count = [], [], {}, {}, [0]

    def run(kernel, outs, *args, smem=0, **options):
        args = list(args)
        if latest or held:
            args[smem] = after(args[smem], *latest, *held)
        done = kernel_call(kernel, outs, *args, smem=smem, **options)
        latest[:] = [jax.tree.leaves(done)[0]]
        held.clear()
        return done

    def main(kernel, *args, **options):
        done = run(kernel, *args, **options)
        count[0] += 1
        return done

    def main_placed(kernel, outs, *args, **options):
        return main(kernel, outs, place, *args, smem=1, **options)

    def step(name):
        def keep(function):
            pending[name] = function
            return function

        return keep

    def need(name):
        if name not in made:
            function = pending.pop(name)
            made[name] = function()
        return made[name]

    def place_of(name):
        return PLACES.get(name, 99)

    def flush():
        for name in sorted(pending, key=place_of):
            if name in pending and place_of(name) <= count[0]:
                need(name)

    def now(value):
        return after(value, *latest)

    def placed(kernel, outs, *args, **options):
        return run(kernel, outs, place, *args, smem=1, **options)

    def scratch_of(*items):
        return [pltpu.VMEM(item.shape, item.dtype) for item in items] + [
            pltpu.SemaphoreType.DMA((len(items),))
        ]

    def picked(one, two, *types):
        return placed(pick_kernel, [shape(one.shape, item) for item in types], one, two, mib=8)

    def collect(chunk):
        got = {step: to_peer(chunk, step, peers) for step in order}
        return [chunk] + [got[step] for step in range(1, peers)]

    def columns(mine, other):
        got = collect(after(mine, *latest))
        return got + [other] + [other_core(item) for item in got[1:]]

    def spread(parts):
        got = {step: to_peer(parts[step], step, peers) for step in order}
        return [parts[0]] + [got[step] for step in range(1, peers)]

    def part_type(step):
        return F32 if step == 0 else BF16

    def gather(half, *before):
        half = after(half, *before)
        return half, along(half, 2) if stepped else lax.all_gather(half, "dp", axis=0, tiled=True)

    def stacked(half, far):
        if not stepped:
            return far, far
        both = run(
            stack_kernel, shape((2 * shard, half.shape[1]), BF16), half, far, mib=4
        )
        return both, along(both, 1)

    def assembled(both, near):
        if not stepped:
            return both
        return placed(
            partial(assemble_kernel, shard), shape((width, both.shape[1]), BF16), both, near, mib=4
        )

    def unpacked(own, items):
        other = other_core(own)
        cols = own.shape[1] // items
        if items == 1:
            outs = shape((2, width, cols), BF16)
        else:
            outs = [shape((3, width, cols), BF16)] + [shape((width // 2, cols), BF16)] * 2
        return placed(unpack_kernel, outs, own, other, mib=8)

    def project(chunk, mix, vec):
        return main(
            project_kernel,
            [shape((rows, heads_width), BF16)] * 3,
            chunk,
            mix,
            vec,
            mib=4,
        )

    def join(projected):
        return main(
            partial(join_kernel, peers),
            [shape((buffer, heads_width), BF16)] * 2,
            *[item[1] for item in projected],
            *[item[2] for item in projected],
            mib=4,
        )

    def attend(step, query, keys, values):
        return main(
            attend_kernel,
            [
                shape((rows, heads_width), F32),
                shape((rows, heads_width), BF16),
                shape((heads, rows, buffer), BF16),
            ],
            query,
            keys,
            values,
            seg_cols[step],
            seg_row,
            mib=8,
        )

    def projections(whole, vec, mix):
        projected = {}
        for item in [0] + take:
            projected[item] = project(whole[item], mix, vec)
            flush()
        return [projected[item] for item in range(peers)]

    def attention(projected):
        keys, values = join(projected)
        flush()
        attended = [None] * peers
        for item in give + [0]:
            attended[item] = attend(item, projected[item][0], keys, values)
            flush()
        query, mixed = [item[0] for item in projected], [item[0] for item in attended]
        kept = (query, keys, values, [item[2] for item in attended], mixed)
        return spread([item[1] for item in attended]), kept

    def middle_norm(hidden, vec, parts, outs):
        return main_placed(
            partial(middle_norm_kernel, peers),
            [shape((rows, width), F32), shape((rows, width), BF16)],
            hidden,
            vec,
            *parts,
            *outs,
            mib=4,
        )

    def forward_inner(step, normed, pair, vec):
        return main(
            forward_inner_kernel,
            [
                shape((rows, width), part_type(step)),
                shape((rows, units), BF16),
                shape((rows, units), F32),
            ],
            normed,
            pair,
            vec,
            mib=8,
        )

    def end_norm(after_rows, vec, next_vec, parts, beside=False):
        return (run if beside else main)(
            partial(end_norm_kernel, peers),
            [shape((rows, width), BF16)] * (1 if next_vec is None else 2),
            after_rows,
            vec,
            vec if next_vec is None else next_vec,
            *parts,
            mib=4,
        )

    def backward_inner(step, delta, pair, slope):
        return main(
            backward_inner_kernel,
            [shape((rows, width), part_type(step)), shape((rows, units), BF16)],
            delta,
            pair,
            slope,
            mib=8,
        )

    def inner_weights(normed, inner_delta, delta, activated):
        return placed(
            partial(inner_weights_kernel, peers),
            [shape((width, units), BF16)] * 2 + [shape((1, units), F32)],
            *normed,
            *inner_delta,
            *delta,
            *activated,
            mib=16,
        )

    def middle_pull(delta, after_rows, vec, parts, outs):
        full, rounded, sums, *pieces = main_placed(
            partial(middle_pull_kernel, peers),
            [shape((rows, width), F32), shape((rows, width), BF16), shape((8, width), F32)]
            + [shape((rows, heads_width), BF16)] * peers,
            delta,
            after_rows,
            vec,
            *parts,
            *outs,
            mib=8,
        )
        return full, rounded, sums, spread(pieces)

    def attention_pull(mix_delta, kept, mix):
        query, keys, values, weights, mixed = kept
        three = main(
            partial(attend_pull_kernel, peers),
            [shape((peers, rows, heads_width), BF16)] * 3,
            keys,
            values,
            *query,
            *mix_delta,
            *weights,
            *mixed,
            scratch=[pltpu.VMEM((heads_width, buffer), F32)] * 2,
            mib=16,
        )
        flush()
        parts = {}
        for item in give + [0]:
            parts[item] = main(
                partial(project_pull_kernel, item),
                shape((rows, width), part_type(item)),
                *three,
                mix,
                mib=4,
            )
            flush()
        return three, spread([parts[item] for item in range(peers)])

    def mix_weights(three, whole, whole_after, mixed):
        return placed(
            partial(mix_weights_kernel, peers),
            [shape((width, 2 * heads_width), BF16)] * 2 + [shape((2, heads_width), F32)],
            *three,
            *whole,
            *whole_after,
            *mixed,
            mib=16,
        )

    def first_pull(after_delta, hidden, vec, parts, dtype):
        return main(
            partial(first_pull_kernel, peers),
            [shape((rows, width), dtype), shape((8, width), F32)],
            after_delta,
            hidden,
            vec,
            *parts,
            mib=8,
        )

    def presummed(kept, got):
        cols = got.shape[1]
        if not stepped:
            both = run(presum_kernel, shape(got.shape, BF16), kept, got, mib=4)
            return [lax.psum_scatter(both, "dp", scatter_dimension=0, tiled=True)]
        held, given = placed(
            partial(presum_shards_kernel, shard),
            [shape((2 * shard, cols), F32), shape((2 * shard, cols), BF16)],
            kept,
            got,
            mib=4,
        )
        return held, along(given, 1)

    def halfway(held, *got):
        if not stepped:
            return [held]
        kept, given = run(
            halfway_kernel,
            [shape((shard, held.shape[1]), F32), shape((shard, held.shape[1]), BF16)],
            held,
            *got,
            mib=4,
        )
        return kept, along(given, 2)

    def settled(parts):
        if not stepped:
            return parts[0].astype(F32)
        return run(final_sum_kernel, shape(parts[0].shape, F32), *parts, mib=4)

    sources = (mix_weight, out_weight)
    mix_own, mix_sent = placed(
        pack_kernel,
        [shape((shard, 2 * heads_width), BF16)] * 2,
        *sources,
        scratch=scratch_of(*sources),
        far=2,
        mib=8,
    )
    mix_got = other_core(mix_sent)
    sources = (tokens, cotangent, norm_gain, row_shift, hidden_bias, up_weight, turned_down)
    entered = run(
        enter_kernel,
        [shape((rows, width), BF16)] * 2
        + [shape((1, buffer), jnp.int32), shape((PACKED, width), F32)]
        + [shape((shard, units), BF16)] * 2
        + [shape((rows, 1), jnp.int32)] * peers,
        place,
        lengths,
        assignment,
        flat_head,
        *sources,
        scratch=scratch_of(*sources),
        smem=3,
        far=7,
        mib=8,
    )
    entering, pushed, seg_row, vec_own, inner_own, inner_sent = entered[:6]
    seg_cols = entered[6:]
    vec_got, inner_got = other_core(vec_own), other_core(inner_sent)
    mix_halves = picked(mix_own, mix_got, BF16, BF16)
    halfway_mix = gather(mix_halves[0])
    vecs = picked(vec_own, vec_got, F32, F32)
    normed = run(first_norm_kernel, shape((rows, width), BF16), entering, vecs[0], mib=4)
    whole_one = collect(normed)
    if SWITCHES["early"]:
        inner_halves = picked(inner_own, inner_got, BF16, BF16)
        halfway_mix = stacked(*halfway_mix)
    else:
        halfway_mix = stacked(*halfway_mix)
        inner_halves = picked(
            after(inner_own, *whole_one[1 : 1 + SWITCHES["first"]]), inner_got, BF16, BF16
        )
    if SWITCHES["early"] > 1:
        inner_far = gather(after(inner_halves[0], *latest))
    mix_one = assembled(
        halfway_mix[0],
        after(halfway_mix[1], *(whole_one[1 : 1 + SWITCHES["first"]] if SWITCHES["early"] else ())),
    )

    def weights(name, half, before, items):
        @step(name + "_far")
        def far():
            if before:
                need(before)
            elif SWITCHES["early"] > 1:
                return inner_far
            return gather(now(half))

        @step(name + "_stack")
        def stack():
            return stacked(*need(name + "_far"))

        @step(name + "_join")
        def joined():
            return assembled(*need(name + "_stack"))

        @step(name)
        def unpack():
            return unpacked(need(name + "_join"), items)

    weights("inner1", inner_halves[0], None, 1)
    weights("mix2", mix_halves[1], "inner1_far", 2)
    weights("inner2", inner_halves[1], "mix2_far", 1)

    @step("push")
    def push():
        return collect(now(after(pushed, *whole_one[1:])))

    def hold(name, first=1):
        @step(name + "_held")
        def keep():
            held.extend(need(name)[first:])

    def gradient(name, parts):
        step(name + "_parts")(parts)

        @step(name + "_given")
        def exchange():
            return other_core(now(need(name + "_parts")[1]))

        @step(name + "_sum")
        def presum():
            given = need(name + "_given")
            return presummed(need(name + "_parts")[0], given)

        @step(name + "_half")
        def half():
            return halfway(*need(name + "_sum"))

        @step(name)
        def total():
            return settled(need(name + "_half"))

        hold(name + "_sum")
        hold(name + "_half")

    hold("push")
    hold("inner1_far")
    hold("mix2_far")
    hold("inner2_far")
    flush()
    mix_one, *out_one = unpacked(mix_one, 2)

    @step("out1")
    def outs_one():
        return columns(*out_one)

    hold("out1")
    flush()
    projected = projections(whole_one, vecs[0], mix_one)
    parts, kept_one = attention(projected)
    after_one, normed = middle_norm(entering, vecs[0], parts, need("out1"))
    whole_inner_one = collect(normed)
    flush()
    pair_one = need("inner1")
    inner_one = {}
    for item in [0] + take:
        inner_one[item] = forward_inner(item, whole_inner_one[item], pair_one, vecs[0])
        flush()
    parts = spread([inner_one[item][0] for item in range(peers)])
    output_one, normed = end_norm(after_one, vecs[0], vecs[1], parts)
    whole_two = collect(normed)
    flush()

    mix_two, *out_two = need("mix2")

    @step("out2")
    def outs_two():
        return columns(*out_two)

    hold("out2")
    flush()
    projected = projections(whole_two, vecs[1], mix_two)
    parts, kept_two = attention(projected)
    after_two, normed = middle_norm(output_one, vecs[1], parts, need("out2"))
    whole_inner_two = collect(normed)
    flush()
    pair_two = need("inner2")
    whole_push = need("push")
    inner_two, pulled = {}, {}
    for item in [0] + take:
        inner_two[item] = forward_inner(item, whole_inner_two[item], pair_two, vecs[1])
        pulled[item] = backward_inner(item, whole_push[item], pair_two, inner_two[item][2])
        flush()
    parts = spread([pulled[item][0] for item in range(peers)])
    pulled_two = pulled

    def inner_weights_two():
        return inner_weights(
            whole_inner_two,
            [pulled_two[item][1] for item in range(peers)],
            whole_push,
            [inner_two[item][1] for item in range(peers)],
        )

    gradient("d_inner2", inner_weights_two)
    flush()
    after_delta, rounded_two, sums_middle, mix_delta = middle_pull(
        pushed, after_two, vecs[1], parts, need("out2")
    )

    mix_delta_two = mix_delta

    @step("after2")
    def whole_after_two():
        return collect(now(after(rounded_two, *mix_delta_two[1 : SWITCHES["calm"]])))


    @step("late")
    def late():
        return spread([now(inner_two[item][0]) for item in range(peers)])

    hold("late")
    @step("late_end")
    def late_end():
        parts = need("late")
        (output_two,) = end_norm(after_two, vecs[1], None, parts, beside=True)
        return picked(output_one, output_two, BF16, BF16)

    @step("late_given")
    def late_given():
        return other_core(now(need("late_end")[1]))

    flush()
    three, parts = attention_pull(mix_delta, kept_two, mix_two)
    three_two = three
    gradient("d_mix2", lambda: mix_weights(three_two, whole_two, need("after2"), kept_two[4]))
    flush()
    delta_two, sums_first = first_pull(after_delta, output_one, vecs[1], parts, BF16)
    sums_two = (sums_first, sums_middle)
    whole_delta = collect(delta_two)
    flush()

    pulled = {}
    for item in [0] + take:
        pulled[item] = backward_inner(item, whole_delta[item], pair_one, inner_one[item][2])
        flush()
    parts = spread([pulled[item][0] for item in range(peers)])
    pulled_one = pulled

    def inner_weights_one():
        return inner_weights(
            whole_inner_one,
            [pulled_one[item][1] for item in range(peers)],
            whole_delta,
            [inner_one[item][1] for item in range(peers)],
        )

    gradient("d_inner1", inner_weights_one)
    flush()
    after_delta, rounded_one, sums_middle, mix_delta = middle_pull(
        delta_two, after_one, vecs[0], parts, need("out1")
    )

    @step("after1")
    def whole_after_one():
        return collect(now(after(rounded_one, *mix_delta[1 : SWITCHES["calm"]])))

    flush()
    three, parts = attention_pull(mix_delta, kept_one, mix_one)
    three_one = three
    gradient("d_mix1", lambda: mix_weights(three_one, whole_one, need("after1"), kept_one[4]))
    flush()
    delta_one, sums_first = first_pull(after_delta, entering, vecs[0], parts, F32)
    sums_one = (sums_first, sums_middle)

    def by_core(kept, got):
        return placed(place_kernel, shape((1, 2) + kept.shape, kept.dtype), kept, got, mib=8)

    @step("sums")
    def sums():
        vectors = []
        for number, layer in (("1", sums_one), ("2", sums_two)):
            vectors += [*layer, need("d_inner" + number + "_parts")[2], need("d_mix" + number + "_parts")[2]]
        kept, given = placed(sums_kernel, [shape((PACKED, width), F32)] * 2, *vectors, mib=4)
        return kept, other_core(given)

    @step("pieces")
    def pieces():
        return placed(
            partial(pieces_kernel, ways, width // (ways * peers), heads),
            shape((ways * peers, 16, 128), F32),
            *need("sums"),
            mib=4,
        )

    @step("shares")
    def shares():
        return run(
            shares_kernel,
            [
                shape((1, 2, width // (ways * peers)), F32),
                shape((1, 4, width // (ways * peers)), F32),
                shape((1, units // 128, 128 // ways), F32),
                shape((1, 2, heads, HEAD_DIM // ways), F32),
            ],
            lax.all_to_all(need("pieces"), ("dp", "tensor"), 0, 0, tiled=True),
            mib=4,
        )

    @step("delta")
    def delta():
        kept, given = picked(delta_one, delta_two, F32, F32)
        return kept, other_core(given)

    @step("delta_out")
    def delta_out():
        return by_core(*need("delta"))

    @step("late_out")
    def late_out():
        return by_core(need("late_end")[0], need("late_given"))

    @step("inner_given")
    def inner_total():
        kept, given = picked(need("d_inner1"), need("d_inner2"), F32, F32)
        return kept, other_core(given)

    @step("inner_out")
    def inner_out():
        return placed(
            inner_out_kernel, [shape((1, shard, units), F32)] * 2, *need("inner_given"), mib=4
        )

    @step("mix_given")
    def mix_total():
        kept, given = picked(need("d_mix1"), need("d_mix2"), F32, F32)
        return kept, other_core(given)

    @step("mix_out")
    def mix_out():
        return placed(
            mix_out_kernel,
            [shape((1, 3, shard, heads_width), F32), shape((1, heads_width, shard), F32)],
            *need("mix_given"),
            mib=4,
        )

    for name in sorted(pending, key=place_of):
        if not name.endswith("_held"):
            need(name)
    gain_gradient, shift_gradient, hidden_gradient, head_gradient = made["shares"]
    layer_output, input_gradient = made["late_out"], made["delta_out"]
    mix_gradient, out_gradient = made["mix_out"]
    up_gradient, down_gradient = made["inner_out"]
    return (
        layer_output,
        input_gradient,
        mix_gradient,
        head_gradient,
        out_gradient,
        gain_gradient,
        shift_gradient,
        up_gradient,
        hidden_gradient,
        jnp.swapaxes(down_gradient, 1, 2),
    )


def solution(mesh):
    placed = (
        P(None, ("dp", "tensor"), None),
        P(None, ("dp", "tensor"), None),
        P("dp", None),
        P("dp", None),
        P("section", None, "dp", "tensor"),
        P("section", None, "tensor", None),
        P("section", "tensor", "dp"),
        P("section", None, None),
        P("section", None, None),
        P("section", "dp", "tensor"),
        P("section", "tensor", None),
        P("section", "tensor", "dp"),
    )
    return jax.shard_map(
        on_device,
        mesh=mesh,
        in_specs=placed,
        out_specs=(
            P("section", None, ("dp", "tensor"), None),
            P("section", None, ("dp", "tensor"), None),
            P("section", None, "dp", "tensor"),
            P("section", None, "tensor", "dp"),
            P("section", "tensor", "dp"),
            P("section", None, ("dp", "tensor")),
            P("section", None, ("dp", "tensor")),
            P("section", "dp", "tensor"),
            P("section", "tensor", "dp"),
            P("section", "tensor", "dp"),
        ),
        check_vma=False,
    )
```
